32 devices in a mesh: seq: 8 (over z, x), fsdp: 4 (over y, core).
Axes of the slice: x: 2, y: 2, z: 4, core: 2. Of those that a mesh axis runs over, the one named last changes fastest.
Arguments:
- x_in: bfloat16 [4, 1024, 2048], P('fsdp', 'seq'), may hold values from -6 to 6
- cotangent: bfloat16 [4, 1024, 2048], P('fsdp', 'seq'), may hold values from -6 to 6
- doc_lengths: int32 [4, 8], P('fsdp'), may hold values from 1 to 897, 1024 in all within a row
- norm_gain: bfloat16 [2048], P('fsdp'), may hold values from 0.099609375 to 1.8984375
- in_weight: bfloat16 [2048, 8192], P('fsdp'), may hold values from -0.125 to 0.125
- conv_weight: bfloat16 [4096, 4], P('fsdp'), may hold values from -3 to 3
- conv_bias: bfloat16 [4096], P('fsdp'), may hold values from -1 to 1
- x_weight: bfloat16 [4096, 160], P('fsdp'), may hold values from -0.09375 to 0.09375
- dt_weight: bfloat16 [4096, 128], P('fsdp'), may hold values from -0.5 to 0.5
- dt_bias: bfloat16 [4096], P('fsdp'), may hold values from -5.5 to -3.5
- a_log: bfloat16 [4096, 16], P('fsdp'), may hold values from -9.1 to 1.4
- skip_weight: bfloat16 [4096], P('fsdp'), may hold values from 0.5 to 1.5
- out_weight: bfloat16 [4096, 2048], P('fsdp'), may hold values from -0.1875 to 0.1875
Outputs:
- block_out: bfloat16 [4, 1024, 2048], P('fsdp', 'seq')
- x_grad: float32 [4, 1024, 2048], P('fsdp', 'seq')
- gain_grad: float32 [2048], P(('seq', 'fsdp'))
- in_grad: float32 [2048, 8192], P(('seq', 'fsdp'))
- conv_w_grad: float32 [4096, 4], P(('seq', 'fsdp'))
- conv_b_grad: float32 [4096], P(('seq', 'fsdp'))
- x_proj_grad: float32 [4096, 160], P(('seq', 'fsdp'))
- dt_grad: float32 [4096, 128], P(('seq', 'fsdp'))
- bias_dt_grad: float32 [4096], P(('seq', 'fsdp'))
- a_log_grad: float32 [4096, 16], P(('seq', 'fsdp'))
- skip_grad: float32 [4096], P(('seq', 'fsdp'))
- out_grad: float32 [4096, 2048], P(('seq', 'fsdp'))
The draws below stay inside these ranges and needn't reach their ends.
Inputs may be any that keep to these rules, and one draw needn't show every extreme that they name: `doc_lengths`: each row lists 8 document lengths in order that sum to 1024; one is exactly 897.
All inputs are finite; a program needn't handle non-finite values.
Results may differ from the reference program's by a relative error of at most 0.009.
Values may be sent and summed in bfloat16 or wider, within the bound.
No kernel may reach another device: no remote copies, remote signals or barrier semaphores. Data moves between devices by JAX's collectives and lax.ppermute only.
A program may use at most 448 MiB of HBM per device.

```python
import math
import jax
import jax.numpy as jnp
import numpy as np
from jax import lax

D = 2048
INNER = 4096
STATE = 16
DT_RANK = 128
CONV = 4
GROUP = 16
NDOCS = 8
BATCH = 4
SEQ_LEN = 1024
LONGEST = 897


def draw_a_log(key, part):
    lowest = math.log(20.0 / SEQ_LEN)
    highest = math.log(4.0)
    return jax.random.uniform(key, (INNER, STATE), jnp.float32, lowest, highest).astype(jnp.bfloat16)


def block_scale(rng, dims, shards, smallest, high):
    level, own = 1.0, jax.random.fold_in(rng, 6)
    for position, blocks in shards:
        draws = jnp.exp(jax.random.uniform(jax.random.fold_in(own, position), (blocks,), jnp.float32, smallest / len(shards), high / len(shards)))
        level = level * jnp.repeat(draws, dims[position] // blocks).reshape([-1 if axis == position else 1 for axis in range(len(dims))])
    return level


def profile(amount, total, bound, lean):
    portions = [(1 << 20) // math.isqrt(standing ** lean) + 1 for standing in range(2, amount + 1)]
    spare, holding = total - bound - (amount - 1), [1] * (amount - 1)
    while spare > 0:
        movable = [i for i in range(amount - 1) if holding[i] < bound]
        whole, remaining = sum([portions[i] for i in movable]), spare
        for i in movable:
            addition = min(bound - holding[i], max(1, remaining * portions[i] // whole), spare)
            holding[i] = holding[i] + addition
            spare = spare - addition
    return np.array([bound] + holding)


def ragged_sizes(stream_key, count, total, most, slope):
    if count == 2:
        one = jax.random.randint(stream_key, (), max(1, total - most), min(most, total - 1) + 1)
        return jnp.stack([one, total - one])
    sizes = jnp.asarray(profile(count, total, most, slope), jnp.int32)
    couples = (count - 1) // 2
    giver, receiver = sizes[1:1 + 2 * couples:2], sizes[2:2 + 2 * couples:2]
    margin = jnp.minimum(giver - 1, most - receiver)
    shifted = jax.random.randint(jax.random.fold_in(stream_key, 1), (couples,), 0, 1 << 20) % (margin + 1)
    sizes = sizes.at[1:1 + 2 * couples:2].set(giver - shifted).at[2:2 + 2 * couples:2].set(receiver + shifted)
    return sizes[jax.random.permutation(jax.random.fold_in(stream_key, 2), count)]


def bell_draw(stream_key, shape, deviation, reach, cuts=(), kind=jnp.bfloat16):
    factor_of = block_scale(stream_key, shape, cuts, -0.22, 0.18) if cuts else 1.0
    values = jax.random.normal(stream_key, shape, jnp.float32) * deviation * factor_of
    return jnp.minimum(jnp.maximum(values, -reach), reach).astype(kind)


def setup_inputs(seed: int = 0) -> dict:
    seeds = jax.random.split(jax.random.key(seed), 14)
    return {
        "x_in": bell_draw(seeds[0], (BATCH, SEQ_LEN, D), 1.0, 6.0, ((0, 4), (1, 8))),
        "cotangent": bell_draw(seeds[1], (BATCH, SEQ_LEN, D), 1.0, 6.0, ((0, 4), (1, 8))),
        "doc_lengths": jax.vmap(lambda own: ragged_sizes(own, NDOCS, SEQ_LEN, LONGEST, 2))(jax.random.split(seeds[2], BATCH)).reshape((BATCH, NDOCS)).astype(jnp.int32),
        "norm_gain": jnp.clip(1.0 + 0.18 * jax.random.normal(seeds[3], (D,), jnp.float32), 0.099609375, 1.8984375).astype(jnp.bfloat16),
        "in_weight": bell_draw(seeds[4], (D, 2 * INNER), D ** -0.5, 0.125, ((0, 4),)),
        "conv_weight": bell_draw(seeds[5], (INNER, CONV), CONV ** -0.5, 3.0, ((0, 4),)),
        "conv_bias": jnp.clip(jax.random.uniform(seeds[6], (INNER,), jnp.float32, -1.0, 1.0) * block_scale(seeds[6], (INNER,), ((0, 4),), -0.4, 0.0), -1.0, 1.0).astype(jnp.bfloat16),
        "x_weight": bell_draw(seeds[7], (INNER, DT_RANK + 2 * STATE), INNER ** -0.5, 0.09375, ((0, 4),)),
        "dt_weight": bell_draw(seeds[8], (INNER, DT_RANK), DT_RANK ** -0.5, 0.5, ((0, 4),)),
        "dt_bias": jnp.clip(-5.5 + 2.0 * jax.random.uniform(seeds[9], (INNER,), jnp.float32) ** block_scale(seeds[9], (INNER,), ((0, 4),), -0.2, 0.2), -5.5, -3.5).astype(jnp.bfloat16),
        "a_log": draw_a_log(jax.random.fold_in(seeds[13], 71), 0),
        "skip_weight": jnp.clip(0.5 + 1.0 * jax.random.uniform(seeds[11], (INNER,), jnp.float32) ** block_scale(seeds[11], (INNER,), ((0, 4),), -0.2, 0.2), 0.5, 1.5).astype(jnp.bfloat16),
        "out_weight": bell_draw(seeds[12], (INNER, D), (INNER // 4) ** -0.5, 0.1875, ((0, 4),)),
    }


NORM_EPS = 1e-05

@jax.custom_vjp
def low(v):
    return lax.optimization_barrier(v.astype(jnp.bfloat16)).astype(jnp.float32)

@jax.custom_vjp
def low_back(v):
    return v

def low_keep(v):
    return (low(v), None)

def low_pass(kept, grad):
    return (grad,)

def back_keep(v):
    return (v, None)

def back_low(kept, grad):
    return (low(grad),)
low.defvjp(low_keep, low_pass)
low_back.defvjp(back_keep, back_low)

def group_step(decay_rate, carry_state, pieces):
    step_c, b_c, c_c, act_c, keep_c = pieces
    running = carry_state
    outputs = []
    for token_place in range(GROUP):
        decay_now = jnp.exp(step_c[token_place][:, None] * decay_rate) * keep_c[token_place]
        drive_now = (step_c[token_place] * act_c[token_place])[:, None] * b_c[token_place][None, :]
        running = decay_now * running + drive_now
        outputs.append(lax.optimization_barrier(jnp.sum(running * c_c[token_place][None, :], axis=1)))
    return (running, jnp.stack(outputs))

def run_scan(start_state, decay_rate, step_size, b_in, c_out, activated, keep_state):
    blocks = step_size.shape[0] // GROUP
    pieces = (step_size.reshape(blocks, GROUP, -1), b_in.reshape(blocks, GROUP, -1), c_out.reshape(blocks, GROUP, -1), activated.reshape(blocks, GROUP, -1), keep_state.reshape(blocks, GROUP))
    checked = jax.checkpoint(group_step)

    def advance(carry_state, one_piece):
        return checked(decay_rate, carry_state, one_piece)
    final_state, outputs = lax.scan(advance, start_state, pieces)
    return (final_state, outputs.reshape(step_size.shape[0], -1))

def doc_masks(lengths, positions):
    doc_ends = jnp.cumsum(lengths).astype(jnp.int32)
    doc_starts = (doc_ends - lengths).astype(jnp.int32)

    def segment_of(places):
        return lax.optimization_barrier(jnp.sum((doc_starts[None, :] <= places[:, None]).astype(jnp.int32), axis=1))
    own_doc = segment_of(positions)
    valid_taps = []
    for offset in range(CONV):
        source = positions - (CONV - 1 - offset)
        valid_taps.append(((source >= 0) & (segment_of(source) == own_doc)).astype(jnp.float32))
    begins = jnp.any(doc_starts[None, :] == positions[:, None], axis=1)
    keep_state = 1.0 - begins.astype(jnp.float32)
    return (jnp.stack(valid_taps), keep_state)

def forward(x_row, params, valid_taps, keep_state):
    gain_vec, w_in, conv_w, conv_b, w_x, w_dt, bias_dt, log_rate, skip_vec, w_out = params
    highest = lax.Precision.HIGHEST
    length = x_row.shape[0]
    inv_rms = lax.rsqrt(lax.optimization_barrier(jnp.mean(x_row * x_row, axis=1, keepdims=True)) + NORM_EPS)
    normed = x_row * inv_rms
    lowered = low(normed * gain_vec)
    projected = low_back(jnp.dot(lowered, w_in, precision=highest))
    conv_in = low(projected[:, :INNER])
    gate_z = projected[:, INNER:]
    padded = jnp.concatenate([jnp.zeros((CONV - 1, INNER), jnp.float32), conv_in], axis=0)
    conv_out = conv_b[None, :]
    for offset in range(CONV):
        conv_out = conv_out + conv_w[:, offset] * padded[offset:offset + length] * valid_taps[offset][:, None]
    activated = low(jax.nn.silu(conv_out))
    mixed_proj = low_back(jnp.dot(activated, w_x, precision=highest))
    low_rank = low(mixed_proj[:, :DT_RANK])
    b_in = mixed_proj[:, DT_RANK:DT_RANK + STATE]
    c_out = mixed_proj[:, DT_RANK + STATE:]
    pre_step = low_back(jnp.dot(low_rank, w_dt.T, precision=highest)) + bias_dt
    step_size = jax.nn.softplus(pre_step)
    decay_rate = -jnp.exp(log_rate)
    final_state, scan_y = run_scan(jnp.zeros((INNER, STATE), jnp.float32), decay_rate, step_size, b_in, c_out, activated, keep_state)
    y_total = scan_y + skip_vec * activated
    branch = low(y_total * jax.nn.silu(gate_z))
    return x_row + jnp.dot(branch, w_out, precision=highest)

def reference(x_in, cotangent, doc_lengths, norm_gain, in_weight, conv_weight, conv_bias, x_weight, dt_weight, dt_bias, a_log, skip_weight, out_weight):
    params = tuple((weight.astype(jnp.float32) for weight in (norm_gain, in_weight, conv_weight, conv_bias, x_weight, dt_weight, dt_bias, a_log, skip_weight, out_weight)))
    positions = jnp.arange(SEQ_LEN, dtype=jnp.int32)

    def one_sequence(totals, pieces_in):
        x_row, cot_row, lengths = pieces_in
        valid_taps, keep_state = doc_masks(lengths, positions)

        def apply_block(x_value, weights):
            return forward(x_value, weights, valid_taps, keep_state)
        result, pullback = jax.vjp(apply_block, x_row.astype(jnp.float32), params)
        row_grad, weight_grads = pullback(cot_row.astype(jnp.float32))
        totals = jax.tree.map(lambda first_sum, second_sum: first_sum + second_sum, totals, weight_grads)
        return (totals, (result.astype(jnp.bfloat16), row_grad))
    zero_grads = jax.tree.map(jnp.zeros_like, params)
    totals, (block_out, x_grad) = lax.scan(one_sequence, zero_grads, (x_in, cotangent, doc_lengths))
    gain_grad, in_grad, conv_w_grad, conv_b_grad, x_proj_grad, dt_grad, bias_dt_grad, a_log_grad, skip_grad, out_grad = totals
    return (block_out, x_grad, gain_grad, in_grad, conv_w_grad, conv_b_grad, x_proj_grad, dt_grad, bias_dt_grad, a_log_grad, skip_grad, out_grad)
```

```python
import jax
import jax.numpy as jnp
from jax import lax
from jax.experimental import pallas as pl
from jax.experimental.pallas import tpu as pltpu
from jax.sharding import PartitionSpec as P

INNER = 4096
STATE = 16
DT_RANK = 128
CONV = 4
MIXED = DT_RANK + 2 * STATE
NORM_EPS = 1e-05
LOG2E = 1.4426950408889634
BLOCK = 128
WIDE = 256
GROUP = 16
RESET = 1e30
VMEM = 56 << 20
F32, BF16 = jnp.float32, jnp.bfloat16


def dot_nn(a, b):
    return lax.dot_general(a, b, (((1,), (0,)), ((), ())), preferred_element_type=F32)


def dot_tn(a, b):
    return lax.dot_general(a, b, (((0,), (0,)), ((), ())), preferred_element_type=F32)


def dot_nt(a, b):
    return lax.dot_general(a, b, (((1,), (1,)), ((), ())), preferred_element_type=F32)


def silu_slope(values):
    sig = jax.nn.sigmoid(values)
    return sig * (1.0 + values * (1.0 - sig))


def softplus(values):
    return jnp.maximum(values, 0.0) + jnp.log1p(jnp.exp(-jnp.abs(values)))


def sigmoid(values):
    return 1.0 / (1.0 + jnp.exp(-values))


ANY = pl.BlockSpec(memory_space=pl.ANY)


def ordered_kernel(*refs):
    pass


def after(value, *others):
    return pl.pallas_call(
        ordered_kernel,
        in_specs=[ANY] * (1 + len(others)),
        out_specs=ANY,
        out_shape=jax.ShapeDtypeStruct(value.shape, value.dtype),
        input_output_aliases={0: 0},
        name="after",
    )(value, *others)


def doc_masks(lengths, count):
    docs = lengths.shape[0]
    order = jnp.arange(docs, dtype=jnp.int32)
    starts = jnp.sum(jnp.where(order[None, :] < order[:, None], lengths[None, :], 0), axis=1)
    places = jnp.arange(count, dtype=jnp.int32)

    def segment_of(at):
        return jnp.sum((starts[None, :] <= at[:, None]).astype(jnp.int32), axis=1)

    own = segment_of(places)
    columns = []
    for k in range(CONV):
        source = places - (CONV - 1 - k)
        columns.append(((source >= 0) & (segment_of(source) == own)).astype(F32))
    columns.append(jnp.any(starts[None, :] == places[:, None], axis=1).astype(F32))
    columns += [jnp.zeros_like(columns[0])] * (8 - len(columns))
    return jnp.stack(columns, axis=1)


ROW_LOG, ROW_CONV, ROW_CONV_B, ROW_DT_B, ROW_SKIP = 0, 16, 20, 21, 22


def assemble_kernel(slots_ref, *refs):
    n = slots_ref.shape[0]
    pieces, (w_ref, gain_ref, gains_ref, w_sem, gain_sem) = refs[:n], refs[n:]
    deep = w_ref.shape[0] // n
    copies = []
    for k, piece in enumerate(pieces):
        slot = slots_ref[k]
        at = pl.multiple_of(slot * deep, deep)
        copies.append(pltpu.make_async_copy(piece.at[:deep], w_ref.at[pl.ds(at, deep)], w_sem.at[k]))
        copies.append(pltpu.make_async_copy(piece.at[deep : deep + GROUP], gains_ref.at[slot], gain_sem.at[k]))
    for copy in copies:
        copy.start()
    for copy in copies:
        copy.wait()
    parts = []
    for i in range(n):
        gains = gains_ref[i].astype(F32)
        lanes = min(deep, gains.shape[1])
        parts += [gains[r : r + 1, :lanes] for r in range(deep // lanes)]
    gain_ref[...] = jnp.concatenate(parts, axis=1)


def assemble(pieces, slots, deep):
    n, columns = len(pieces), pieces[0].shape[1]
    return pl.pallas_call(
        assemble_kernel,
        in_specs=[pl.BlockSpec(memory_space=pltpu.SMEM), *[ANY] * n],
        out_specs=[pl.BlockSpec(memory_space=pltpu.VMEM)] * 2,
        out_shape=[jax.ShapeDtypeStruct((n * deep, columns), BF16), jax.ShapeDtypeStruct((1, n * deep), F32)],
        scratch_shapes=[
            pltpu.VMEM((n, GROUP, columns), BF16),
            pltpu.SemaphoreType.DMA((n,)),
            pltpu.SemaphoreType.DMA((n,)),
        ],
        compiler_params=pltpu.CompilerParams(vmem_limit_bytes=VMEM),
        name="assemble",
    )(slots, *pieces)


def project_kernel(slots_ref, w_in_ref, gain_ref, w_xt_ref, table_ref, mask_ref, *refs):
    n = slots_ref.shape[0]
    pieces = refs[:n]
    (lowered_ref, conv_in_ref, conv_out_ref, act_ref, gate_ref, mixed_ref, line_ref, x_ref, x_sem) = refs[n:]
    rows, width = conv_in_ref.shape
    block = pl.program_id(0)
    tokens = pieces[0].shape[0]

    @pl.when(block == 0)
    def _():
        for k, piece in enumerate(pieces):
            slot = slots_ref[k]
            pltpu.make_async_copy(piece, x_ref.at[slot], x_sem.at[slot]).start()
        line_ref[:8] = jnp.zeros((8, width), F32)

    @pl.when(block > 0)
    def _():
        line_ref[:8] = line_ref[rows:]

    per = rows // tokens
    for i in range(per):
        slot = block * per + i
        pltpu.make_async_copy(pieces[0], x_ref.at[slot], x_sem.at[slot]).wait()
    x = jnp.concatenate([x_ref[block * per + i] for i in range(per)], axis=0).astype(F32)
    inv = lax.rsqrt(jnp.mean(x * x, axis=1, keepdims=True) + NORM_EPS)
    lowered_ref[...] = (x * inv * gain_ref[...]).astype(BF16)
    projected = dot_nn(lowered_ref[...], w_in_ref[...])
    conv_in = projected[:, :width].astype(BF16)
    gate_ref[...] = projected[:, width:]
    conv_in_ref[...] = conv_in
    line_ref[8:] = conv_in.astype(F32)
    conv_out = table_ref[ROW_CONV_B : ROW_CONV_B + 1, :]
    for k in range(CONV):
        taps = table_ref[ROW_CONV + k : ROW_CONV + k + 1, :]
        conv_out = conv_out + taps * line_ref[5 + k : 5 + k + rows] * mask_ref[:, k : k + 1]
    conv_out_ref[...] = conv_out
    act = (conv_out * sigmoid(conv_out)).astype(BF16)
    act_ref[...] = act
    mixed = dot_nt(w_xt_ref[...], act).astype(BF16)
    for i in range(rows // BLOCK):
        mixed_ref[i] = mixed[:, i * BLOCK : (i + 1) * BLOCK]


def rows_spec(width, index=lambda i: i, rows=BLOCK):
    return pl.BlockSpec((rows, width), lambda i: (index(i), 0))


def whole_spec(shape):
    return pl.BlockSpec(shape, lambda i: (0,) * len(shape))


def project(pieces, slots, w_rows, gain, w_xt, table, mask):
    tokens, model = pieces[0].shape
    count = tokens * len(pieces)
    width = w_xt.shape[1]

    def rows(columns):
        return rows_spec(columns, rows=WIDE)

    return pl.pallas_call(
        project_kernel,
        grid=(count // WIDE,),
        in_specs=[
            pl.BlockSpec(memory_space=pltpu.SMEM), whole_spec(w_rows.shape), whole_spec(gain.shape),
            whole_spec(w_xt.shape), whole_spec(table.shape), rows(8), *[ANY] * len(pieces),
        ],
        out_specs=[
            rows(model), rows(width), rows(width), rows(width), rows(width),
            pl.BlockSpec((WIDE // BLOCK, MIXED, BLOCK), lambda i: (i, 0, 0)),
        ],
        out_shape=[
            jax.ShapeDtypeStruct((count, model), BF16),
            jax.ShapeDtypeStruct((count, width), BF16),
            jax.ShapeDtypeStruct((count, width), F32),
            jax.ShapeDtypeStruct((count, width), BF16),
            jax.ShapeDtypeStruct((count, width), F32),
            jax.ShapeDtypeStruct((count // BLOCK, MIXED, BLOCK), BF16),
        ],
        scratch_shapes=[
            pltpu.VMEM((WIDE + 8, width), F32),
            pltpu.VMEM((len(pieces), tokens, model), BF16),
            pltpu.SemaphoreType.DMA((len(pieces),)),
        ],
        compiler_params=pltpu.CompilerParams(vmem_limit_bytes=VMEM),
        cost_estimate=pl.CostEstimate(flops=2 * count * model * 2 * width, bytes_accessed=20 << 20, transcendentals=0),
        name="project",
    )(slots, w_rows, gain, w_xt, table, mask, *pieces)


def spread_groups(values):
    state = lax.broadcasted_iota(jnp.int32, (STATE, GROUP * STATE), 0)
    column = lax.broadcasted_iota(jnp.int32, (STATE, GROUP * STATE), 1)
    pick = jnp.where((column & (STATE - 1)) == state, 1.0, 0.0).astype(BF16)
    tiled = dot_tn(values, pick)
    token = lax.broadcasted_iota(jnp.int32, (BLOCK, GROUP * STATE), 0)
    column = lax.broadcasted_iota(jnp.int32, (BLOCK, GROUP * STATE), 1)
    return jnp.where((token & (GROUP - 1)) == (column >> 4), tiled, 0.0).astype(BF16)


def spread_lanes(values, own_ref, out_ref):
    ones = jnp.ones((BLOCK, BLOCK), BF16)
    for g in range(BLOCK // GROUP):
        here = slice(g * GROUP * STATE, (g + 1) * GROUP * STATE)
        out_ref[here] = dot_nn(jnp.concatenate([values] * GROUP, axis=0) * own_ref[here], ones)


def wide(values, width):
    lanes = values.shape[1]
    return values[:, :width] if width < lanes else jnp.concatenate([values] * (width // lanes), axis=1)


def owns():
    row, column = (lax.broadcasted_iota(jnp.int32, (BLOCK * STATE, BLOCK), i) for i in (0, 1))
    ahead = column - row // STATE
    return (ahead == 0).astype(BF16), ahead[: GROUP * STATE]


def forward_kernel(mixed_ref, act_ref, gate_ref, mask_ref, w_dtt_ref, table_ref, own_ref, _,
                   branch_ref, y_ref, states_ref, _out, h_ref, stepd_ref, drive_ref, b_ref):
    @pl.when(pl.program_id(0) == 0)
    def _():
        h_ref[...] = jnp.zeros_like(h_ref)

    width = act_ref.shape[1]
    act = act_ref[...].astype(F32)
    pre = dot_tn(mixed_ref[0, :DT_RANK], w_dtt_ref[...]) + table_ref[ROW_DT_B : ROW_DT_B + 1, :]
    step = softplus(pre)
    stepd_ref[...] = jnp.where(mask_ref[:, CONV : CONV + 1] > 0.0, RESET, step)
    drive_ref[...] = step * act
    spread_lanes(mixed_ref[0, DT_RANK : DT_RANK + STATE], own_ref, b_ref)
    rate = -jnp.exp(table_ref[ROW_LOG : ROW_LOG + STATE, :]) * LOG2E

    def group(g, h):
        r0 = pl.multiple_of(g * GROUP, GROUP)
        stepd = stepd_ref[pl.ds(r0, GROUP), :]
        drive = drive_ref[pl.ds(r0, GROUP), :]
        for j in range(GROUP):
            at = pl.multiple_of((r0 + j) * STATE, STATE)
            b = wide(b_ref[pl.ds(at, STATE), :], width)
            h = jnp.exp2(stepd[j : j + 1, :] * rate) * h + drive[j : j + 1, :] * b
            states_ref[pl.ds(at, STATE), :] = h.astype(BF16)
        return h

    h_ref[...] = lax.fori_loop(0, BLOCK // GROUP, group, h_ref[...])
    c = spread_groups(mixed_ref[0, DT_RANK + STATE :])
    for g in range(BLOCK // GROUP):
        at = g * GROUP
        y_ref[at : at + GROUP, :] = dot_nn(c[at : at + GROUP], states_ref[at * STATE : (at + GROUP) * STATE])
    y_total = y_ref[...] + table_ref[ROW_SKIP : ROW_SKIP + 1, :] * act
    y_ref[...] = y_total
    gate = gate_ref[...]
    branch_ref[...] = (y_total * (gate * sigmoid(gate))).astype(BF16)


def scan_forward(mixed, act, gate, mask, w_dtt, table, own, w_out):
    count, width = act.shape
    return pl.pallas_call(
        forward_kernel,
        grid=(count // BLOCK,),
        in_specs=[
            pl.BlockSpec((1, MIXED, BLOCK), lambda i: (i, 0, 0)), rows_spec(width), rows_spec(width), rows_spec(8),
            whole_spec(w_dtt.shape), whole_spec(table.shape), whole_spec(own.shape), ANY,
        ],
        out_specs=[rows_spec(width), rows_spec(width), pl.BlockSpec((BLOCK * STATE, width), lambda i: (i, 0)), ANY],
        out_shape=[
            jax.ShapeDtypeStruct((count, width), BF16),
            jax.ShapeDtypeStruct((count, width), F32),
            jax.ShapeDtypeStruct((count * STATE, width), BF16),
            jax.ShapeDtypeStruct(w_out.shape, w_out.dtype),
        ],
        input_output_aliases={7: 3},
        scratch_shapes=[
            pltpu.VMEM((STATE, width), F32),
            pltpu.VMEM((BLOCK, width), F32),
            pltpu.VMEM((BLOCK, width), F32),
            pltpu.VMEM((BLOCK * STATE, BLOCK), F32),
        ],
        compiler_params=pltpu.CompilerParams(vmem_limit_bytes=VMEM),
        cost_estimate=pl.CostEstimate(flops=8 * count * width * STATE * 16, bytes_accessed=64 << 20, transcendentals=0),
        name="scan_forward",
    )(mixed, act, gate, mask, w_dtt, table, own, w_out)


def backward_kernel(mixed_ref, act_ref, gate_ref, d_branch_ref, mask_ref, states_ref, ahead_ref,
                    w_dtt_ref, table_ref, own_ref, offset_ref,
                    d_mixed_ref, d_act_ref, sums_ref, dt_grad_ref,
                    p_ref, dy_ref, stepd_ref, c_ref, s1_ref, s2_ref, bg_ref, dyt_ref, sat_ref, d_b_ref, d_c_ref,
                    adj_a_ref, adj_b_ref, rq_a_ref, rq_b_ref):
    first = pl.program_id(0) == 0
    width = act_ref.shape[1]

    @pl.when(first)
    def _():
        p_ref[...] = jnp.zeros_like(p_ref)
        sums_ref[...] = jnp.zeros_like(sums_ref)
        dt_grad_ref[...] = jnp.zeros_like(dt_grad_ref)
        adj_b_ref[...] = jnp.zeros_like(adj_b_ref)
        rq_b_ref[...] = jnp.zeros_like(rq_b_ref)
        d_b_ref[...] = jnp.zeros_like(d_b_ref)
        d_c_ref[...] = jnp.zeros_like(d_c_ref)
        bg_ref[BLOCK:] = jnp.zeros((GROUP, GROUP * STATE), BF16)

    act = act_ref[...].astype(F32)
    gate = gate_ref[...]
    sig = sigmoid(gate)
    d_branch = d_branch_ref[...]
    dy = d_branch * (gate * sig)
    pre = dot_tn(mixed_ref[0, :DT_RANK], w_dtt_ref[...]) + table_ref[ROW_DT_B : ROW_DT_B + 1, :]
    step = softplus(pre)
    dy_ref[...] = dy
    stepd_ref[...] = jnp.where(mask_ref[:, CONV : CONV + 1] > 0.0, RESET, step)
    dyt_ref[...] = dy.T.astype(BF16)
    sat_ref[...] = (step * act).T.astype(BF16)
    spread_lanes(mixed_ref[0, DT_RANK + STATE :], own_ref, c_ref)
    bg_ref[:BLOCK] = spread_groups(mixed_ref[0, DT_RANK : DT_RANK + STATE])
    raw = -jnp.exp(table_ref[ROW_LOG : ROW_LOG + STATE, :])
    rate = raw * LOG2E
    groups = BLOCK // GROUP
    per = GROUP * STATE
    token = lax.broadcasted_iota(jnp.int32, (GROUP, per), 0)
    column = lax.broadcasted_iota(jnp.int32, (GROUP, per), 1)
    ones = jnp.where(token == (column >> 4), 1.0, 0.0).astype(BF16)
    pick = jnp.where(token == (column & (STATE - 1)), 1.0, 0.0).astype(BF16)

    def steps(g, p, total, adj_ref, rq_ref):
        r0 = pl.multiple_of(g * GROUP, GROUP)
        dy_g = dy_ref[pl.ds(r0, GROUP), :]
        stepd_g = stepd_ref[pl.ds(r0, GROUP), :]
        for j in reversed(range(GROUP)):
            at = pl.multiple_of((r0 + j) * STATE, STATE)
            if j:
                behind = pl.multiple_of((r0 + j - 1) * STATE, STATE)
                before = states_ref[pl.ds(behind, STATE), :]
            else:
                behind = pl.multiple_of(jnp.maximum(r0 - 1, 0) * STATE, STATE)
                before = jnp.where(g > 0, states_ref[pl.ds(behind, STATE), :], ahead_ref[...])
            adj = dy_g[j : j + 1, :] * wide(c_ref[pl.ds(at, STATE), :], width) + p
            adj_ref[j * STATE : (j + 1) * STATE] = adj.astype(BF16)
            p = jnp.exp2(stepd_g[j : j + 1, :] * rate) * adj
            rq = raw * (p * before.astype(F32))
            rq_ref[j * STATE : (j + 1) * STATE] = rq.astype(BF16)
            total = total + stepd_g[j : j + 1, :] * rq
        return p, total

    def sums(g, state_rows, adj_ref, rq_ref):
        r0 = pl.multiple_of(g * GROUP, GROUP)
        adj = adj_ref[...]
        s1_ref[pl.ds(r0, GROUP), :] = dot_nn(bg_ref[pl.ds(r0, GROUP), :], adj)
        s2_ref[pl.ds(r0, GROUP), :] = dot_nn(ones, rq_ref[...])
        here = offset_ref[...] == r0
        d_b_ref[...] = jnp.where(here, dot_nn(adj, sat_ref[...]), d_b_ref[...])
        states = states_ref[pl.ds(state_rows, per), :]
        d_c_ref[...] = jnp.where(here, dot_nn(states, dyt_ref[...]), d_c_ref[...])

    def pair(i, carry):
        p, total = carry
        high = groups - 1 - 2 * i
        low = high - 1
        rows = pl.multiple_of(jnp.minimum(low + 2, groups - 1) * per, per)
        sums(low + 2, rows, adj_b_ref, rq_b_ref)
        p, total = steps(high, p, total, adj_a_ref, rq_a_ref)
        sums(high, pl.multiple_of(high * per, per), adj_a_ref, rq_a_ref)
        return steps(low, p, total, adj_b_ref, rq_b_ref)

    p, total = lax.fori_loop(0, groups // 2, pair, (p_ref[...], sums_ref[:STATE]))
    sums(0, 0, adj_b_ref, rq_b_ref)
    p_ref[...] = p
    sums_ref[:STATE] = total
    d_mixed_ref[0, DT_RANK : DT_RANK + STATE] = dot_nn(pick, d_b_ref[...].astype(BF16)).astype(BF16)
    d_mixed_ref[0, DT_RANK + STATE :] = dot_nn(pick, d_c_ref[...].astype(BF16)).astype(BF16)

    s1, s2 = s1_ref[:BLOCK], s2_ref[:BLOCK]
    d_act_ref[...] = dy * table_ref[ROW_SKIP : ROW_SKIP + 1, :] + step * s1
    d_pre = (act * s1 + s2) * jnp.exp(pre - step)
    sums_ref[STATE : STATE + 1] += jnp.sum(dy * act, axis=0, keepdims=True)
    sums_ref[STATE + 1 : STATE + 2] += jnp.sum(d_pre, axis=0, keepdims=True)
    d_pre = d_pre.astype(BF16)
    dt_grad_ref[...] += dot_nn(mixed_ref[0, :DT_RANK], d_pre)
    d_mixed_ref[0, :DT_RANK] = dot_nt(w_dtt_ref[...], d_pre).astype(BF16)


def scan_backward(mixed, act, gate, d_branch, mask, states, w_dtt, table, own, offsets):
    count, width = act.shape
    blocks = count // BLOCK
    last = blocks - 1
    rows = rows_spec(width, lambda i: last - i)
    mixed_spec = pl.BlockSpec((1, MIXED, BLOCK), lambda i: (last - i, 0, 0))
    per = GROUP * STATE
    return pl.pallas_call(
        backward_kernel,
        grid=(blocks,),
        in_specs=[
            mixed_spec, rows, rows, rows, rows_spec(8, lambda i: last - i),
            pl.BlockSpec((BLOCK * STATE, width), lambda i: (last - i, 0)),
            pl.BlockSpec((STATE, width), lambda i: (jnp.maximum((last - i) * BLOCK - 1, 0), 0)),
            whole_spec(w_dtt.shape), whole_spec(table.shape), whole_spec(own.shape), whole_spec(offsets.shape),
        ],
        out_specs=[mixed_spec, rows, whole_spec((24, width)), whole_spec((DT_RANK, width))],
        out_shape=[
            jax.ShapeDtypeStruct((blocks, MIXED, BLOCK), BF16),
            jax.ShapeDtypeStruct((count, width), F32),
            jax.ShapeDtypeStruct((24, width), F32),
            jax.ShapeDtypeStruct((DT_RANK, width), F32),
        ],
        scratch_shapes=[
            pltpu.VMEM((STATE, width), F32),
            pltpu.VMEM((BLOCK, width), F32),
            pltpu.VMEM((BLOCK, width), F32),
            pltpu.VMEM((BLOCK * STATE, BLOCK), F32),
            pltpu.VMEM((BLOCK + GROUP, width), F32),
            pltpu.VMEM((BLOCK + GROUP, width), F32),
            pltpu.VMEM((BLOCK + GROUP, per), BF16),
            pltpu.VMEM((width, BLOCK), BF16),
            pltpu.VMEM((width, BLOCK), BF16),
            pltpu.VMEM((per, BLOCK), F32),
            pltpu.VMEM((per, BLOCK), F32),
            pltpu.VMEM((per, width), BF16),
            pltpu.VMEM((per, width), BF16),
            pltpu.VMEM((per, width), BF16),
            pltpu.VMEM((per, width), BF16),
        ],
        compiler_params=pltpu.CompilerParams(vmem_limit_bytes=VMEM),
        cost_estimate=pl.CostEstimate(flops=8 * count * width * STATE * 32, bytes_accessed=96 << 20, transcendentals=0),
        name="scan_backward",
    )(mixed, act, gate, d_branch, mask, states, states, w_dtt, table, own, offsets)


def finish_kernel(mixed_ref, d_act_ref, conv_out_ref, conv_in_ref, ahead_ref, act_ref, d_gate_ref, mask_ref, w_xt_ref,
                  table_ref, d_proj_ref, x_grad_ref, sums_ref, line_ref, masked_ref):
    first = pl.program_id(0) == 0
    rows, width = act_ref.shape

    @pl.when(first)
    def _():
        x_grad_ref[...] = jnp.zeros_like(x_grad_ref)
        sums_ref[...] = jnp.zeros_like(sums_ref)
        for k in range(CONV - 1):
            masked_ref[k, rows:] = jnp.zeros((8, width), F32)

    @pl.when(jnp.logical_not(first))
    def _():
        for k in range(CONV - 1):
            masked_ref[k, rows:] = masked_ref[k, :8]

    mixed = jnp.concatenate([mixed_ref[i] for i in range(rows // BLOCK)], axis=1)
    x_grad_ref[...] += dot_nn(mixed, act_ref[...])
    d_act = d_act_ref[...] + dot_tn(mixed, w_xt_ref[...])
    conv_out = conv_out_ref[...]
    sig = sigmoid(conv_out)
    d_conv = d_act * (sig * (1.0 + conv_out * (1.0 - sig)))
    sums_ref[CONV : CONV + 1] += jnp.sum(d_conv, axis=0, keepdims=True)
    line_ref[:8] = ahead_ref[...].astype(F32)[8:]
    line_ref[8:] = conv_in_ref[...].astype(F32)
    d_conv_in = jnp.zeros((rows, width), F32)
    for k in range(CONV):
        masked = d_conv * mask_ref[:, k : k + 1]
        sums_ref[k : k + 1] += jnp.sum(masked * line_ref[5 + k : 5 + k + rows], axis=0, keepdims=True)
        if k < CONV - 1:
            masked_ref[k, :rows] = masked
            masked = masked_ref[k, CONV - 1 - k : CONV - 1 - k + rows]
        d_conv_in = d_conv_in + table_ref[ROW_CONV + k : ROW_CONV + k + 1, :] * masked
    d_proj_ref[:, :width] = d_conv_in.astype(BF16)
    d_proj_ref[:, width:] = d_gate_ref[...]


def finish(mixed, d_act, conv_out, conv_in, act, d_gate, mask, w_xt, table):
    count, width = act.shape
    blocks = count // WIDE
    last = blocks - 1

    def rows(columns):
        return rows_spec(columns, lambda i: last - i, WIDE)

    per = WIDE // GROUP
    return pl.pallas_call(
        finish_kernel,
        grid=(blocks,),
        in_specs=[
            pl.BlockSpec((WIDE // BLOCK, MIXED, BLOCK), lambda i: (last - i, 0, 0)), rows(width), rows(width), rows(width),
            pl.BlockSpec((GROUP, width), lambda i: (jnp.maximum((last - i) * per - 1, 0), 0)),
            rows(width), rows(width), rows(8), whole_spec(w_xt.shape), whole_spec(table.shape),
        ],
        out_specs=[rows(2 * width), whole_spec((MIXED, width)), whole_spec((8, width))],
        out_shape=[
            jax.ShapeDtypeStruct((count, 2 * width), BF16),
            jax.ShapeDtypeStruct((MIXED, width), F32),
            jax.ShapeDtypeStruct((8, width), F32),
        ],
        scratch_shapes=[pltpu.VMEM((WIDE + 8, width), F32), pltpu.VMEM((CONV - 1, WIDE + 8, width), F32)],
        compiler_params=pltpu.CompilerParams(vmem_limit_bytes=VMEM),
        cost_estimate=pl.CostEstimate(flops=1 << 31, bytes_accessed=12 << 20, transcendentals=0),
        name="finish",
    )(mixed, d_act, conv_out, conv_in, conv_in, act, d_gate, mask, w_xt, table)


def lower_kernel(where_ref, d_proj_ref, w_ref, _, *out_refs):
    row, column = where_ref[0], where_ref[1]
    tokens = out_refs[0].shape[0]
    mine, theirs = out_refs[:4], out_refs[4:]
    for i, k in enumerate((1, 2, 3, 0)):
        at = lax.rem(row - k + 4, 4) * 2
        parts = [d_proj_ref[pl.ds(pl.multiple_of((at + column) * tokens, tokens), tokens), :]]
        if i:
            parts.append(d_proj_ref[pl.ds(pl.multiple_of((at + 1 - column) * tokens, tokens), tokens), :])
        out = dot_nt(jnp.concatenate(parts, axis=0), w_ref[...]).astype(BF16)
        mine[i][...] = out[:tokens]
        if i:
            theirs[i - 1][...] = out[tokens:]


def lower(where, d_proj, w_rows, first):
    tokens, model = first.shape
    vmem = pl.BlockSpec(memory_space=pltpu.VMEM)
    out = pl.pallas_call(
        lower_kernel,
        in_specs=[pl.BlockSpec(memory_space=pltpu.SMEM), vmem, vmem, ANY],
        out_specs=[vmem] * 7,
        out_shape=[jax.ShapeDtypeStruct((tokens, model), BF16)] * 7,
        compiler_params=pltpu.CompilerParams(vmem_limit_bytes=VMEM),
        cost_estimate=pl.CostEstimate(flops=2 * d_proj.size * model, bytes_accessed=12 << 20, transcendentals=0),
        name="lower",
    )(where.astype(jnp.int32), d_proj, w_rows, first)
    return out[:4], out[4:]


def line_ring(seqs):
    return [(i, (i + 2) % seqs) for i in range(seqs)]


def pair_swap(size, bit):
    return [(i, i ^ bit) for i in range(size)]


def gather_all(part, shard):
    seqs, shards = lax.axis_size("seq"), lax.axis_size("fsdp")
    if (seqs, shards) != (8, 4):
        whole, wide = lax.all_gather(part, "seq", axis=0), lax.all_gather(shard, "fsdp", axis=0)
        return (
            [whole[k] for k in range(seqs)], jnp.arange(seqs, dtype=jnp.int32),
            [wide[k] for k in range(shards)], jnp.arange(shards, dtype=jnp.int32),
        )
    place, here = lax.axis_index("seq"), lax.axis_index("fsdp")
    row, column = place // 2, place % 2
    swap, ring = pair_swap(seqs, 1), line_ring(seqs)
    pieces, slots = [], []
    far = lax.ppermute(shard, "fsdp", pair_swap(shards, 2))
    beside = lax.ppermute(shard, "fsdp", pair_swap(shards, 1))
    for k in range(4):
        slot = (row - k + 4) % 4 * 2
        swapped = lax.ppermute(part, "seq", swap)
        pieces += [part, swapped]
        slots += [slot + column, slot + 1 - column]
        if k == 3:
            break
        part = lax.ppermute(part, "seq", ring)
        if k == 0:
            part = after(part, swapped)
        elif k == 1:
            part = after(part, swapped, beside)
            far = after(far, part)
            both = lax.ppermute(far, "fsdp", pair_swap(shards, 1))
        else:
            part = after(part, swapped, both)
    w_slots = jnp.stack([here, here ^ 2, here ^ 1, here ^ 3]).astype(jnp.int32)
    return pieces, jnp.stack(slots).astype(jnp.int32), [shard, far, beside, both], w_slots


def sum_over_seq(part):
    seqs = lax.axis_size("seq")
    shares = part.reshape((seqs, part.shape[0] // seqs) + part.shape[1:])
    shares = lax.all_to_all(shares, "seq", split_axis=0, concat_axis=0, tiled=True)
    total = jnp.sum(shares.astype(F32), axis=0).astype(BF16)
    copies = jnp.broadcast_to(total, shares.shape)
    return lax.all_to_all(copies, "seq", split_axis=0, concat_axis=0, tiled=True).reshape(part.shape), total


def from_owner(shares, owner):
    seqs, shards = lax.axis_size("seq"), lax.axis_size("fsdp")
    here = lax.axis_index("fsdp")
    if (seqs, shards) != (8, 4):
        every = jnp.stack([shares(j) for j in range(shards)])
        every = lax.dynamic_index_in_dim(lax.all_gather(every, "fsdp"), owner, 0, False)
        return [lax.dynamic_index_in_dim(every, here, 0, False)]
    got = [jnp.where(here == owner, shares(here), 0)]
    for j in range(1, shards):
        pairs = [(s * shards + s * shards // seqs, s * shards + (s * shards // seqs ^ j)) for s in range(seqs)]
        got.append(lax.ppermute(shares(here ^ j), ("seq", "fsdp"), pairs))
    return got


def scatter_shards(blocks, kind=BF16):
    shards = lax.axis_size("fsdp")
    if shards != 4 or lax.axis_size("seq") != 8:
        return lax.psum_scatter(blocks, "fsdp", scatter_dimension=0)
    here = lax.axis_index("fsdp")
    total = lax.dynamic_index_in_dim(blocks, here, 0, False).astype(F32)
    for j in range(1, shards):
        theirs = lax.dynamic_index_in_dim(blocks, here ^ j, 0, False).astype(kind)
        total = total + lax.ppermute(theirs, "fsdp", pair_swap(shards, j)).astype(F32)
    return total


def local(
    x_in, cotangent, doc_lengths, norm_gain, in_weight, conv_weight, conv_bias,
    x_weight, dt_weight, dt_bias, a_log, skip_weight, out_weight,
):
    seqs, shards = lax.axis_size("seq"), lax.axis_size("fsdp")
    place = lax.axis_index("seq")
    width = INNER // seqs
    tokens, model = x_in.shape[1:]
    count = tokens * seqs
    deep = model // shards

    held = INNER // shards
    owner, offset = place * width // held, place * width % held
    lanes = min(2 * width, deep)
    small = jnp.concatenate(
        [
            dt_weight.T, a_log.T, conv_weight.T, conv_bias[None], dt_bias[None], skip_weight[None],
            jnp.zeros((MIXED - DT_RANK - STATE - CONV - 3, held), BF16),
        ],
        axis=0,
    )
    small = jnp.concatenate(
        [lax.dynamic_slice_in_dim(x_weight.T, offset, width, 1), lax.dynamic_slice_in_dim(small, offset, width, 1)], axis=1
    )
    gain_rows = norm_gain.reshape(-1, lanes)
    gain_rows = jnp.pad(gain_rows, ((0, GROUP - gain_rows.shape[0]), (0, 2 * width - lanes)))
    in_cols = jnp.concatenate(
        [
            lax.dynamic_slice_in_dim(in_weight, place * width, width, 1),
            lax.dynamic_slice_in_dim(in_weight, INNER + place * width, width, 1),
        ],
        axis=1,
    )
    shard = jnp.concatenate([in_cols, gain_rows, small], axis=0)
    pieces, slots, w_pieces, w_slots = gather_all(x_in[0], shard)
    small = sum(jnp.where(w_slots[k] == owner, piece[deep + GROUP :], 0) for k, piece in enumerate(w_pieces))
    w_xt, w_dtt, table = small[:, :width], small[:DT_RANK, width:], small[DT_RANK:, width:].astype(F32)
    cot_all = lax.all_gather(after(cotangent[0], pieces[-2]), "seq", axis=0, tiled=True)
    rows = model // (seqs * shards)
    start = place * shards * rows % deep
    in_got = from_owner(
        lambda j: after(lax.dynamic_slice_in_dim(in_weight, start + j * rows, rows, 0), pieces[2]), owner
    )
    out_rows = after(lax.dynamic_slice_in_dim(out_weight, offset, width, 0), pieces[-2])
    out_got = from_owner(lambda j: out_rows, owner)
    mask = doc_masks(doc_lengths[0], count)

    own, offsets = owns()
    w_rows, gain = assemble(w_pieces, w_slots, deep)
    lowered, conv_in, conv_out, act, gate, mixed = project(pieces, slots, w_rows, gain, w_xt, table, mask)
    mixed, share = sum_over_seq(mixed)
    in_rows = sum(in_got[1:], after(in_got[0], share))
    w_out = sum(out_got[1:], after(out_got[0], share))
    mixed = after(mixed, in_rows)
    branch, y_total, states, w_out = scan_forward(mixed, act, gate, mask, w_dtt, table, own, w_out)
    block_part = dot_nn(branch, w_out).astype(BF16)
    block_sum = lax.psum_scatter(block_part, "seq", scatter_dimension=0, tiled=True)
    block_out = (x_in[0].astype(F32) + block_sum.astype(F32)).astype(BF16)

    d_branch = dot_nt(cot_all, w_out)
    d_gate = (d_branch * y_total * silu_slope(gate)).astype(BF16)
    d_branch = after(d_branch, block_part, d_gate)
    d_mixed, d_act, sums, dt_grad = scan_backward(
        mixed, act, gate, d_branch, mask, states, w_dtt, table, own, offsets
    )
    out_grad = scatter_shards(dot_tn(branch, cot_all).reshape(shards, width // shards, model))

    def shared(part):
        return scatter_shards(part.reshape(seqs, shards, rows, width).transpose(1, 0, 2, 3)).astype(BF16)

    def spread(part):
        part = lax.all_to_all(part, "seq", split_axis=0, concat_axis=0, tiled=True)
        return part.transpose(1, 0, 2).reshape(rows, INNER).astype(F32)

    gate_sum = shared(dot_tn(lowered, d_gate))
    d_mixed, share = sum_over_seq(d_mixed)
    d_mixed = after(d_mixed, block_sum)
    gate_grad = spread(after(gate_sum, share))
    d_proj, x_proj_grad, conv_sums = finish(d_mixed, d_act, conv_out, conv_in, act, d_gate, mask, w_xt, table)

    small = jnp.concatenate([x_proj_grad, dt_grad, sums, conv_sums], axis=0)
    if seqs == 8:
        row, column = place // 2, place % 2
        swap, ring = pair_swap(seqs, 1), line_ring(seqs)
        first = (row + 3) % 4 * 2 + 1 - column
        first = dot_nt(lax.dynamic_slice_in_dim(d_proj, first * tokens, tokens, 0), w_rows).astype(BF16)
        swapped = [lax.ppermute(first, "seq", swap)]
        mine, theirs = lower(jnp.stack([row, column]), d_proj, w_rows, first)
        conv_sum = shared(dot_tn(lowered, after(d_proj, *theirs)[:, :width]))
        swapped += [lax.ppermute(block, "seq", swap) for block in theirs]
        total = mine[0].astype(F32) + swapped[0].astype(F32)
        befores = (theirs, (gate_grad,), (conv_sum,))
        for k in range(3):
            total = after(total.astype(BF16), *befores[k])
            if k == 2:
                small = after(small, total)
            total = lax.ppermute(total, "seq", ring).astype(F32) + mine[k + 1].astype(F32) + swapped[k + 1].astype(F32)
        d_low_own = total
    else:
        conv_sum = shared(dot_tn(lowered, d_proj[:, :width]))
        d_lowered = dot_nt(d_proj, w_rows).astype(BF16)
        d_low_own = lax.psum_scatter(d_lowered, "seq", scatter_dimension=0, tiled=True).astype(F32)
    conv_grad = spread(conv_sum)

    x_own = x_in[0].astype(F32)
    inv_own = lax.rsqrt(jnp.mean(x_own * x_own, axis=1, keepdims=True) + NORM_EPS)
    normed_own = x_own * inv_own
    d_norm = d_low_own * gain
    x_grad = cotangent[0].astype(F32) + inv_own * (
        d_norm - normed_own * jnp.mean(d_norm * normed_own, axis=1, keepdims=True)
    )
    in_grad = jnp.concatenate([conv_grad, gate_grad], axis=1)
    gain_own = lax.dynamic_slice_in_dim(gain[0], (place * shards + lax.axis_index("fsdp")) * rows, rows, 0)
    gain_grad = jnp.sum(in_grad * in_rows.astype(F32), axis=1) / gain_own
    small = small.reshape(-1, shards, width // shards).transpose(1, 0, 2)
    small = scatter_shards(small, F32)
    at = MIXED + DT_RANK
    tail = at + 24
    return (
        block_out[None],
        x_grad[None],
        gain_grad,
        in_grad,
        small[tail : tail + CONV].T,
        small[tail + CONV],
        small[:MIXED].T,
        small[MIXED:at].T,
        small[at + STATE + 1],
        small[at : at + STATE].T,
        small[at + STATE],
        out_grad,
    )


def solution(mesh):
    by_row, by_vec = P("fsdp", None), P("fsdp")
    tok = P("fsdp", "seq", None)
    out_row, out_vec = P(("seq", "fsdp"), None), P(("seq", "fsdp"))
    in_specs = (
        tok, tok, by_row, by_vec, by_row, by_row, by_vec, by_row, by_row, by_vec, by_row, by_vec, by_row,
    )
    out_specs = (
        tok, tok, out_vec, out_row, out_row, out_vec, out_row, out_row, out_vec, out_row, out_vec, out_row,
    )
    return jax.shard_map(local, mesh=mesh, in_specs=in_specs, out_specs=out_specs, check_vma=False)
```

```python
import jax
import jax.numpy as jnp
from jax import lax
from jax.experimental import pallas as pl
from jax.experimental.pallas import tpu as pltpu
from jax.sharding import PartitionSpec as P

INNER = 4096
STATE = 16
DT_RANK = 128
CONV = 4
MIXED = DT_RANK + 2 * STATE
NORM_EPS = 1e-05
LOG2E = 1.4426950408889634
BLOCK = 128
WIDE = 256
GROUP = 16
RESET = 1e30
VMEM = 56 << 20
F32, BF16 = jnp.float32, jnp.bfloat16


def dot_nn(a, b):
    return lax.dot_general(a, b, (((1,), (0,)), ((), ())), preferred_element_type=F32)


def dot_tn(a, b):
    return lax.dot_general(a, b, (((0,), (0,)), ((), ())), preferred_element_type=F32)


def dot_nt(a, b):
    return lax.dot_general(a, b, (((1,), (1,)), ((), ())), preferred_element_type=F32)


def silu_slope(values):
    sig = jax.nn.sigmoid(values)
    return sig * (1.0 + values * (1.0 - sig))


def softplus(values):
    return jnp.maximum(values, 0.0) + jnp.log1p(jnp.exp(-jnp.abs(values)))


def sigmoid(values):
    return 1.0 / (1.0 + jnp.exp(-values))


ANY = pl.BlockSpec(memory_space=pl.ANY)


def ordered_kernel(*refs):
    pass


def after(value, *others):
    return pl.pallas_call(
        ordered_kernel,
        in_specs=[ANY] * (1 + len(others)),
        out_specs=ANY,
        out_shape=jax.ShapeDtypeStruct(value.shape, value.dtype),
        input_output_aliases={0: 0},
        name="after",
    )(value, *others)


def doc_masks(lengths, count):
    docs = lengths.shape[0]
    order = jnp.arange(docs, dtype=jnp.int32)
    starts = jnp.sum(jnp.where(order[None, :] < order[:, None], lengths[None, :], 0), axis=1)
    places = jnp.arange(count, dtype=jnp.int32)

    def segment_of(at):
        return jnp.sum((starts[None, :] <= at[:, None]).astype(jnp.int32), axis=1)

    own = segment_of(places)
    columns = []
    for k in range(CONV):
        source = places - (CONV - 1 - k)
        columns.append(((source >= 0) & (segment_of(source) == own)).astype(F32))
    columns.append(jnp.any(starts[None, :] == places[:, None], axis=1).astype(F32))
    columns += [jnp.zeros_like(columns[0])] * (8 - len(columns))
    return jnp.stack(columns, axis=1)


ROW_LOG, ROW_CONV, ROW_CONV_B, ROW_DT_B, ROW_SKIP = 0, 16, 20, 21, 22


def assemble_kernel(pieces_ref, w_ref, gain_ref, gains_ref, w_sem, gain_sem):
    n = pieces_ref.shape[0]
    deep = w_ref.shape[0] // n
    copies = []
    for k in range(n):
        piece = pieces_ref.at[k]
        copies.append(pltpu.make_async_copy(piece.at[:deep], w_ref.at[k * deep : (k + 1) * deep], w_sem.at[k]))
        copies.append(pltpu.make_async_copy(piece.at[deep : deep + GROUP], gains_ref.at[k], gain_sem.at[k]))
    for copy in copies:
        copy.start()
    for copy in copies:
        copy.wait()
    parts = []
    for i in range(n):
        gains = gains_ref[i].astype(F32)
        lanes = min(deep, gains.shape[1])
        parts += [gains[r : r + 1, :lanes] for r in range(deep // lanes)]
    gain_ref[...] = jnp.concatenate(parts, axis=1)


def assemble(pieces, deep):
    n, _, columns = pieces.shape
    return pl.pallas_call(
        assemble_kernel,
        in_specs=[ANY],
        out_specs=[pl.BlockSpec(memory_space=pltpu.VMEM)] * 2,
        out_shape=[jax.ShapeDtypeStruct((n * deep, columns), BF16), jax.ShapeDtypeStruct((1, n * deep), F32)],
        scratch_shapes=[
            pltpu.VMEM((n, GROUP, columns), BF16),
            pltpu.SemaphoreType.DMA((n,)),
            pltpu.SemaphoreType.DMA((n,)),
        ],
        compiler_params=pltpu.CompilerParams(vmem_limit_bytes=VMEM),
        name="assemble",
    )(pieces)


def project_kernel(slots_ref, w_in_ref, gain_ref, w_xt_ref, table_ref, mask_ref, *refs):
    n = slots_ref.shape[0]
    pieces = refs[:n]
    (lowered_ref, conv_in_ref, conv_out_ref, act_ref, gate_ref, mixed_ref, line_ref, x_ref, x_sem) = refs[n:]
    rows, width = conv_in_ref.shape
    block = pl.program_id(0)
    tokens = pieces[0].shape[0]

    @pl.when(block == 0)
    def _():
        for k, piece in enumerate(pieces):
            slot = slots_ref[k]
            pltpu.make_async_copy(piece, x_ref.at[slot], x_sem.at[slot]).start()
        line_ref[:8] = jnp.zeros((8, width), F32)

    @pl.when(block > 0)
    def _():
        line_ref[:8] = line_ref[rows:]

    per = rows // tokens
    for i in range(per):
        slot = block * per + i
        pltpu.make_async_copy(pieces[0], x_ref.at[slot], x_sem.at[slot]).wait()
    x = jnp.concatenate([x_ref[block * per + i] for i in range(per)], axis=0).astype(F32)
    inv = lax.rsqrt(jnp.mean(x * x, axis=1, keepdims=True) + NORM_EPS)
    lowered_ref[...] = (x * inv * gain_ref[...]).astype(BF16)
    projected = dot_nn(lowered_ref[...], w_in_ref[...])
    conv_in = projected[:, :width].astype(BF16)
    gate_ref[...] = projected[:, width:]
    conv_in_ref[...] = conv_in
    line_ref[8:] = conv_in.astype(F32)
    conv_out = table_ref[ROW_CONV_B : ROW_CONV_B + 1, :]
    for k in range(CONV):
        taps = table_ref[ROW_CONV + k : ROW_CONV + k + 1, :]
        conv_out = conv_out + taps * line_ref[5 + k : 5 + k + rows] * mask_ref[:, k : k + 1]
    conv_out_ref[...] = conv_out
    act = (conv_out * sigmoid(conv_out)).astype(BF16)
    act_ref[...] = act
    mixed = dot_nt(w_xt_ref[...], act).astype(BF16)
    for i in range(rows // BLOCK):
        mixed_ref[i] = mixed[:, i * BLOCK : (i + 1) * BLOCK]


def rows_spec(width, index=lambda i: i, rows=BLOCK):
    return pl.BlockSpec((rows, width), lambda i: (index(i), 0))


def whole_spec(shape):
    return pl.BlockSpec(shape, lambda i: (0,) * len(shape))


def project(pieces, slots, w_rows, gain, w_xt, table, mask):
    tokens, model = pieces[0].shape
    count = tokens * len(pieces)
    width = w_xt.shape[1]

    def rows(columns):
        return rows_spec(columns, rows=WIDE)

    return pl.pallas_call(
        project_kernel,
        grid=(count // WIDE,),
        in_specs=[
            pl.BlockSpec(memory_space=pltpu.SMEM), whole_spec(w_rows.shape), whole_spec(gain.shape),
            whole_spec(w_xt.shape), whole_spec(table.shape), rows(8), *[ANY] * len(pieces),
        ],
        out_specs=[
            rows(model), rows(width), rows(width), rows(width), rows(width),
            pl.BlockSpec((WIDE // BLOCK, MIXED, BLOCK), lambda i: (i, 0, 0)),
        ],
        out_shape=[
            jax.ShapeDtypeStruct((count, model), BF16),
            jax.ShapeDtypeStruct((count, width), BF16),
            jax.ShapeDtypeStruct((count, width), F32),
            jax.ShapeDtypeStruct((count, width), BF16),
            jax.ShapeDtypeStruct((count, width), F32),
            jax.ShapeDtypeStruct((count // BLOCK, MIXED, BLOCK), BF16),
        ],
        scratch_shapes=[
            pltpu.VMEM((WIDE + 8, width), F32),
            pltpu.VMEM((len(pieces), tokens, model), BF16),
            pltpu.SemaphoreType.DMA((len(pieces),)),
        ],
        compiler_params=pltpu.CompilerParams(vmem_limit_bytes=VMEM),
        cost_estimate=pl.CostEstimate(flops=2 * count * model * 2 * width, bytes_accessed=20 << 20, transcendentals=0),
        name="project",
    )(slots, w_rows, gain, w_xt, table, mask, *pieces)


def spread_groups(values):
    state = lax.broadcasted_iota(jnp.int32, (STATE, GROUP * STATE), 0)
    column = lax.broadcasted_iota(jnp.int32, (STATE, GROUP * STATE), 1)
    pick = jnp.where((column & (STATE - 1)) == state, 1.0, 0.0).astype(BF16)
    tiled = dot_tn(values, pick)
    token = lax.broadcasted_iota(jnp.int32, (BLOCK, GROUP * STATE), 0)
    column = lax.broadcasted_iota(jnp.int32, (BLOCK, GROUP * STATE), 1)
    return jnp.where((token & (GROUP - 1)) == (column >> 4), tiled, 0.0).astype(BF16)


def spread_lanes(values, own_ref, out_ref):
    ones = jnp.ones((BLOCK, BLOCK), BF16)
    for g in range(BLOCK // GROUP):
        here = slice(g * GROUP * STATE, (g + 1) * GROUP * STATE)
        out_ref[here] = dot_nn(jnp.concatenate([values] * GROUP, axis=0) * own_ref[here], ones)


def wide(values, width):
    lanes = values.shape[1]
    return values[:, :width] if width < lanes else jnp.concatenate([values] * (width // lanes), axis=1)


def owns():
    row, column = (lax.broadcasted_iota(jnp.int32, (BLOCK * STATE, BLOCK), i) for i in (0, 1))
    ahead = column - row // STATE
    return (ahead == 0).astype(BF16), ahead[: GROUP * STATE]


def forward_kernel(mixed_ref, act_ref, gate_ref, mask_ref, w_dtt_ref, table_ref, own_ref,
                   branch_ref, y_ref, states_ref, h_ref, stepd_ref, drive_ref, b_ref):
    @pl.when(pl.program_id(0) == 0)
    def _():
        h_ref[...] = jnp.zeros_like(h_ref)

    width = act_ref.shape[1]
    act = act_ref[...].astype(F32)
    pre = dot_tn(mixed_ref[0, :DT_RANK], w_dtt_ref[...]) + table_ref[ROW_DT_B : ROW_DT_B + 1, :]
    step = softplus(pre)
    stepd_ref[...] = jnp.where(mask_ref[:, CONV : CONV + 1] > 0.0, RESET, step)
    drive_ref[...] = step * act
    spread_lanes(mixed_ref[0, DT_RANK : DT_RANK + STATE], own_ref, b_ref)
    rate = -jnp.exp(table_ref[ROW_LOG : ROW_LOG + STATE, :]) * LOG2E

    def group(g, h):
        r0 = pl.multiple_of(g * GROUP, GROUP)
        stepd = stepd_ref[pl.ds(r0, GROUP), :]
        drive = drive_ref[pl.ds(r0, GROUP), :]
        for j in range(GROUP):
            at = pl.multiple_of((r0 + j) * STATE, STATE)
            b = wide(b_ref[pl.ds(at, STATE), :], width)
            h = jnp.exp2(stepd[j : j + 1, :] * rate) * h + drive[j : j + 1, :] * b
            states_ref[pl.ds(at, STATE), :] = h.astype(BF16)
        return h

    h_ref[...] = lax.fori_loop(0, BLOCK // GROUP, group, h_ref[...])
    c = spread_groups(mixed_ref[0, DT_RANK + STATE :])
    for g in range(BLOCK // GROUP):
        at = g * GROUP
        y_ref[at : at + GROUP, :] = dot_nn(c[at : at + GROUP], states_ref[at * STATE : (at + GROUP) * STATE])
    y_total = y_ref[...] + table_ref[ROW_SKIP : ROW_SKIP + 1, :] * act
    y_ref[...] = y_total
    gate = gate_ref[...]
    branch_ref[...] = (y_total * (gate * sigmoid(gate))).astype(BF16)


def scan_forward(mixed, act, gate, mask, w_dtt, table, own):
    count, width = act.shape
    return pl.pallas_call(
        forward_kernel,
        grid=(count // BLOCK,),
        in_specs=[
            pl.BlockSpec((1, MIXED, BLOCK), lambda i: (i, 0, 0)), rows_spec(width), rows_spec(width), rows_spec(8),
            whole_spec(w_dtt.shape), whole_spec(table.shape), whole_spec(own.shape),
        ],
        out_specs=[rows_spec(width), rows_spec(width), pl.BlockSpec((BLOCK * STATE, width), lambda i: (i, 0))],
        out_shape=[
            jax.ShapeDtypeStruct((count, width), BF16),
            jax.ShapeDtypeStruct((count, width), F32),
            jax.ShapeDtypeStruct((count * STATE, width), BF16),
        ],
        scratch_shapes=[
            pltpu.VMEM((STATE, width), F32),
            pltpu.VMEM((BLOCK, width), F32),
            pltpu.VMEM((BLOCK, width), F32),
            pltpu.VMEM((BLOCK * STATE, BLOCK), F32),
        ],
        compiler_params=pltpu.CompilerParams(vmem_limit_bytes=VMEM),
        cost_estimate=pl.CostEstimate(flops=8 * count * width * STATE * 16, bytes_accessed=64 << 20, transcendentals=0),
        name="scan_forward",
    )(mixed, act, gate, mask, w_dtt, table, own)


def backward_kernel(mixed_ref, act_ref, gate_ref, d_branch_ref, mask_ref, states_ref, ahead_ref,
                    w_dtt_ref, table_ref, own_ref, offset_ref, _block, _gate,
                    d_mixed_ref, d_act_ref, sums_ref, dt_grad_ref,
                    p_ref, dy_ref, stepd_ref, c_ref, s1_ref, s2_ref, bg_ref, dyt_ref, sat_ref, d_b_ref, d_c_ref,
                    adj_a_ref, adj_b_ref, rq_a_ref, rq_b_ref):
    first = pl.program_id(0) == 0
    width = act_ref.shape[1]

    @pl.when(first)
    def _():
        p_ref[...] = jnp.zeros_like(p_ref)
        sums_ref[...] = jnp.zeros_like(sums_ref)
        dt_grad_ref[...] = jnp.zeros_like(dt_grad_ref)
        adj_b_ref[...] = jnp.zeros_like(adj_b_ref)
        rq_b_ref[...] = jnp.zeros_like(rq_b_ref)
        d_b_ref[...] = jnp.zeros_like(d_b_ref)
        d_c_ref[...] = jnp.zeros_like(d_c_ref)
        bg_ref[BLOCK:] = jnp.zeros((GROUP, GROUP * STATE), BF16)

    act = act_ref[...].astype(F32)
    gate = gate_ref[...]
    sig = sigmoid(gate)
    d_branch = d_branch_ref[...]
    dy = d_branch * (gate * sig)
    pre = dot_tn(mixed_ref[0, :DT_RANK], w_dtt_ref[...]) + table_ref[ROW_DT_B : ROW_DT_B + 1, :]
    step = softplus(pre)
    dy_ref[...] = dy
    stepd_ref[...] = jnp.where(mask_ref[:, CONV : CONV + 1] > 0.0, RESET, step)
    dyt_ref[...] = dy.T.astype(BF16)
    sat_ref[...] = (step * act).T.astype(BF16)
    spread_lanes(mixed_ref[0, DT_RANK + STATE :], own_ref, c_ref)
    bg_ref[:BLOCK] = spread_groups(mixed_ref[0, DT_RANK : DT_RANK + STATE])
    raw = -jnp.exp(table_ref[ROW_LOG : ROW_LOG + STATE, :])
    rate = raw * LOG2E
    groups = BLOCK // GROUP
    per = GROUP * STATE
    token = lax.broadcasted_iota(jnp.int32, (GROUP, per), 0)
    column = lax.broadcasted_iota(jnp.int32, (GROUP, per), 1)
    ones = jnp.where(token == (column >> 4), 1.0, 0.0).astype(BF16)
    pick = jnp.where(token == (column & (STATE - 1)), 1.0, 0.0).astype(BF16)

    def steps(g, p, total, adj_ref, rq_ref):
        r0 = pl.multiple_of(g * GROUP, GROUP)
        dy_g = dy_ref[pl.ds(r0, GROUP), :]
        stepd_g = stepd_ref[pl.ds(r0, GROUP), :]
        for j in reversed(range(GROUP)):
            at = pl.multiple_of((r0 + j) * STATE, STATE)
            if j:
                behind = pl.multiple_of((r0 + j - 1) * STATE, STATE)
                before = states_ref[pl.ds(behind, STATE), :]
            else:
                behind = pl.multiple_of(jnp.maximum(r0 - 1, 0) * STATE, STATE)
                before = jnp.where(g > 0, states_ref[pl.ds(behind, STATE), :], ahead_ref[...])
            adj = dy_g[j : j + 1, :] * wide(c_ref[pl.ds(at, STATE), :], width) + p
            adj_ref[j * STATE : (j + 1) * STATE] = adj.astype(BF16)
            p = jnp.exp2(stepd_g[j : j + 1, :] * rate) * adj
            rq = raw * (p * before.astype(F32))
            rq_ref[j * STATE : (j + 1) * STATE] = rq.astype(BF16)
            total = total + stepd_g[j : j + 1, :] * rq
        return p, total

    def sums(g, state_rows, adj_ref, rq_ref):
        r0 = pl.multiple_of(g * GROUP, GROUP)
        adj = adj_ref[...]
        s1_ref[pl.ds(r0, GROUP), :] = dot_nn(bg_ref[pl.ds(r0, GROUP), :], adj)
        s2_ref[pl.ds(r0, GROUP), :] = dot_nn(ones, rq_ref[...])
        here = offset_ref[...] == r0
        d_b_ref[...] = jnp.where(here, dot_nn(adj, sat_ref[...]), d_b_ref[...])
        states = states_ref[pl.ds(state_rows, per), :]
        d_c_ref[...] = jnp.where(here, dot_nn(states, dyt_ref[...]), d_c_ref[...])

    def pair(i, carry):
        p, total = carry
        high = groups - 1 - 2 * i
        low = high - 1
        rows = pl.multiple_of(jnp.minimum(low + 2, groups - 1) * per, per)
        sums(low + 2, rows, adj_b_ref, rq_b_ref)
        p, total = steps(high, p, total, adj_a_ref, rq_a_ref)
        sums(high, pl.multiple_of(high * per, per), adj_a_ref, rq_a_ref)
        return steps(low, p, total, adj_b_ref, rq_b_ref)

    p, total = lax.fori_loop(0, groups // 2, pair, (p_ref[...], sums_ref[:STATE]))
    sums(0, 0, adj_b_ref, rq_b_ref)
    p_ref[...] = p
    sums_ref[:STATE] = total
    d_mixed_ref[0, DT_RANK : DT_RANK + STATE] = dot_nn(pick, d_b_ref[...].astype(BF16)).astype(BF16)
    d_mixed_ref[0, DT_RANK + STATE :] = dot_nn(pick, d_c_ref[...].astype(BF16)).astype(BF16)

    s1, s2 = s1_ref[:BLOCK], s2_ref[:BLOCK]
    d_act_ref[...] = dy * table_ref[ROW_SKIP : ROW_SKIP + 1, :] + step * s1
    d_pre = (act * s1 + s2) * jnp.exp(pre - step)
    sums_ref[STATE : STATE + 1] += jnp.sum(dy * act, axis=0, keepdims=True)
    sums_ref[STATE + 1 : STATE + 2] += jnp.sum(d_pre, axis=0, keepdims=True)
    d_pre = d_pre.astype(BF16)
    dt_grad_ref[...] += dot_nn(mixed_ref[0, :DT_RANK], d_pre)
    d_mixed_ref[0, :DT_RANK] = dot_nt(w_dtt_ref[...], d_pre).astype(BF16)


def scan_backward(mixed, act, gate, d_branch, mask, states, w_dtt, table, own, offsets, *before):
    count, width = act.shape
    blocks = count // BLOCK
    last = blocks - 1
    rows = rows_spec(width, lambda i: last - i)
    mixed_spec = pl.BlockSpec((1, MIXED, BLOCK), lambda i: (last - i, 0, 0))
    per = GROUP * STATE
    return pl.pallas_call(
        backward_kernel,
        grid=(blocks,),
        in_specs=[
            mixed_spec, rows, rows, rows, rows_spec(8, lambda i: last - i),
            pl.BlockSpec((BLOCK * STATE, width), lambda i: (last - i, 0)),
            pl.BlockSpec((STATE, width), lambda i: (jnp.maximum((last - i) * BLOCK - 1, 0), 0)),
            whole_spec(w_dtt.shape), whole_spec(table.shape), whole_spec(own.shape), whole_spec(offsets.shape), ANY, ANY,
        ],
        out_specs=[mixed_spec, rows, whole_spec((24, width)), whole_spec((DT_RANK, width))],
        out_shape=[
            jax.ShapeDtypeStruct((blocks, MIXED, BLOCK), BF16),
            jax.ShapeDtypeStruct((count, width), F32),
            jax.ShapeDtypeStruct((24, width), F32),
            jax.ShapeDtypeStruct((DT_RANK, width), F32),
        ],
        scratch_shapes=[
            pltpu.VMEM((STATE, width), F32),
            pltpu.VMEM((BLOCK, width), F32),
            pltpu.VMEM((BLOCK, width), F32),
            pltpu.VMEM((BLOCK * STATE, BLOCK), F32),
            pltpu.VMEM((BLOCK + GROUP, width), F32),
            pltpu.VMEM((BLOCK + GROUP, width), F32),
            pltpu.VMEM((BLOCK + GROUP, per), BF16),
            pltpu.VMEM((width, BLOCK), BF16),
            pltpu.VMEM((width, BLOCK), BF16),
            pltpu.VMEM((per, BLOCK), F32),
            pltpu.VMEM((per, BLOCK), F32),
            pltpu.VMEM((per, width), BF16),
            pltpu.VMEM((per, width), BF16),
            pltpu.VMEM((per, width), BF16),
            pltpu.VMEM((per, width), BF16),
        ],
        compiler_params=pltpu.CompilerParams(vmem_limit_bytes=VMEM),
        cost_estimate=pl.CostEstimate(flops=8 * count * width * STATE * 32, bytes_accessed=96 << 20, transcendentals=0),
        name="scan_backward",
    )(mixed, act, gate, d_branch, mask, states, states, w_dtt, table, own, offsets, *before)


def finish_kernel(mixed_ref, d_act_ref, conv_out_ref, conv_in_ref, ahead_ref, act_ref, d_gate_ref, mask_ref, w_xt_ref,
                  table_ref, d_proj_ref, x_grad_ref, sums_ref, line_ref, masked_ref):
    rows, width = act_ref.shape
    d_conv_in = conv_backward(
        (mixed_ref, d_act_ref, conv_out_ref, conv_in_ref, ahead_ref, act_ref, mask_ref, w_xt_ref, table_ref,
         x_grad_ref, sums_ref, line_ref, masked_ref), rows, width, pl.program_id(0) == 0
    )
    d_proj_ref[:, :width] = d_conv_in.astype(BF16)
    d_proj_ref[:, width:] = d_gate_ref[...]


def finish(mixed, d_act, conv_out, conv_in, act, d_gate, mask, w_xt, table):
    count, width = act.shape
    blocks = count // WIDE
    last = blocks - 1

    def rows(columns):
        return rows_spec(columns, lambda i: last - i, WIDE)

    per = WIDE // GROUP
    return pl.pallas_call(
        finish_kernel,
        grid=(blocks,),
        in_specs=[
            pl.BlockSpec((WIDE // BLOCK, MIXED, BLOCK), lambda i: (last - i, 0, 0)), rows(width), rows(width), rows(width),
            pl.BlockSpec((GROUP, width), lambda i: (jnp.maximum((last - i) * per - 1, 0), 0)),
            rows(width), rows(width), rows(8), whole_spec(w_xt.shape), whole_spec(table.shape),
        ],
        out_specs=[rows(2 * width), whole_spec((MIXED, width)), whole_spec((8, width))],
        out_shape=[
            jax.ShapeDtypeStruct((count, 2 * width), BF16),
            jax.ShapeDtypeStruct((MIXED, width), F32),
            jax.ShapeDtypeStruct((8, width), F32),
        ],
        scratch_shapes=[pltpu.VMEM((WIDE + 8, width), F32), pltpu.VMEM((CONV - 1, WIDE + 8, width), F32)],
        compiler_params=pltpu.CompilerParams(vmem_limit_bytes=VMEM),
        cost_estimate=pl.CostEstimate(flops=1 << 31, bytes_accessed=12 << 20, transcendentals=0),
        name="finish",
    )(mixed, d_act, conv_out, conv_in, conv_in, act, d_gate, mask, w_xt, table)


def conv_backward(refs, rows, width, first):
    (mixed_ref, d_act_ref, conv_out_ref, conv_in_ref, ahead_ref, act_ref, mask_ref, w_xt_ref, table_ref,
     x_grad_ref, sums_ref, line_ref, masked_ref) = refs

    @pl.when(first)
    def _():
        x_grad_ref[...] = jnp.zeros_like(x_grad_ref)
        sums_ref[...] = jnp.zeros_like(sums_ref)
        for k in range(CONV - 1):
            masked_ref[k, rows:] = jnp.zeros((8, width), F32)

    @pl.when(jnp.logical_not(first))
    def _():
        for k in range(CONV - 1):
            masked_ref[k, rows:] = masked_ref[k, :8]

    mixed = jnp.concatenate([mixed_ref[i] for i in range(rows // BLOCK)], axis=1)
    x_grad_ref[...] += dot_nn(mixed, act_ref[...])
    d_act = d_act_ref[...] + dot_tn(mixed, w_xt_ref[...])
    conv_out = conv_out_ref[...]
    sig = sigmoid(conv_out)
    d_conv = d_act * (sig * (1.0 + conv_out * (1.0 - sig)))
    sums_ref[CONV : CONV + 1] += jnp.sum(d_conv, axis=0, keepdims=True)
    line_ref[:8] = ahead_ref[...].astype(F32)[8:]
    line_ref[8:] = conv_in_ref[...].astype(F32)
    d_conv_in = jnp.zeros((rows, width), F32)
    for k in range(CONV):
        masked = d_conv * mask_ref[:, k : k + 1]
        sums_ref[k : k + 1] += jnp.sum(masked * line_ref[5 + k : 5 + k + rows], axis=0, keepdims=True)
        if k < CONV - 1:
            masked_ref[k, :rows] = masked
            masked = masked_ref[k, CONV - 1 - k : CONV - 1 - k + rows]
        d_conv_in = d_conv_in + table_ref[ROW_CONV + k : ROW_CONV + k + 1, :] * masked
    return d_conv_in


def tail_kernel(where_ref, mixed_ref, d_act_ref, conv_out_ref, conv_in_ref, ahead_ref, act_ref, d_gate_ref, mask_ref,
                w_xt_ref, table_ref, w_any, lowered_any, *refs):
    mine, theirs, part_ref = refs[:4], refs[4:8], refs[8]
    (x_grad_ref, sums_ref, line_ref, masked_ref, w_ref, lowered_ref, d_conv_ref, gain_ref,
     sem_ref) = refs[9:]
    step = pl.program_id(0)
    rows, width = act_ref.shape
    tokens, model = mine[0].shape
    row, column = where_ref[0], where_ref[1]
    block = pl.num_programs(0) - 1 - step
    w_copy = pltpu.make_async_copy(w_any, w_ref, sem_ref.at[0])
    lowered_copy = pltpu.make_async_copy(lowered_any, lowered_ref, sem_ref.at[1])

    @pl.when(step == 0)
    def _():
        w_copy.start()
        lowered_copy.start()
        gain_ref[...] = jnp.zeros_like(gain_ref)

    d_conv_in = conv_backward(
        (mixed_ref, d_act_ref, conv_out_ref, conv_in_ref, ahead_ref, act_ref, mask_ref, w_xt_ref, table_ref,
         x_grad_ref, sums_ref, line_ref, masked_ref), rows, width, step == 0
    ).astype(BF16)
    at = pl.multiple_of(block * rows, rows)
    d_conv_ref[pl.ds(at, rows), :] = d_conv_in

    @pl.when(step == 0)
    def _():
        w_copy.wait()
        lowered_copy.wait()

    d_proj = jnp.concatenate([d_conv_in, d_gate_ref[...]], axis=1)
    out = dot_nt(d_proj, w_ref[...])
    gain_ref[...] += jnp.sum(out * lowered_ref[pl.ds(at, rows), :].astype(F32), axis=0, keepdims=True)
    halves = out[:tokens].astype(BF16), out[tokens:].astype(BF16)
    k = lax.rem(row - block + 4, 4)
    for j in range(4):
        for c in range(2):

            @pl.when(jnp.logical_and(k == j, column == c))
            def _(j=j, c=c):
                mine[j][...] = halves[c]
                theirs[j][...] = halves[1 - c]

    @pl.when(block == 0)
    def _():
        shards, places, each, _ = part_ref.shape
        each = each - 8
        many = shards * each

        def one(s, carry):
            lanes = pl.ds(pl.multiple_of(s * many, many), many)
            chunk = dot_tn(lowered_ref[:, lanes], d_conv_ref[...]).astype(BF16)
            gains = jnp.broadcast_to(gain_ref[:, lanes], (8, many)).astype(BF16)
            for j in range(shards):
                part_ref[j, s, :each] = chunk[j * each : (j + 1) * each]
                part_ref[j, s, each:] = jnp.concatenate([gains] * (width // many), axis=1)
            return carry

        lax.fori_loop(0, places, one, 0)


def tail(where, mixed, d_act, conv_out, conv_in, act, d_gate, mask, w_xt, table, w_rows, lowered, seqs, shards):
    count, width = act.shape
    model = lowered.shape[1]
    tokens, many = count // seqs, model // seqs
    blocks = count // (2 * tokens)
    last = blocks - 1
    per = 2 * tokens // GROUP

    def rows(columns):
        return pl.BlockSpec((2 * tokens, columns), lambda i: (last - i, 0))

    shapes = [jax.ShapeDtypeStruct((tokens, model), BF16)] * 8
    shapes += [jax.ShapeDtypeStruct((shards, seqs, many // shards + 8, width), BF16)]
    shapes += [jax.ShapeDtypeStruct((MIXED, width), F32), jax.ShapeDtypeStruct((8, width), F32)]
    out = pl.pallas_call(
        tail_kernel,
        grid=(blocks,),
        in_specs=[
            pl.BlockSpec(memory_space=pltpu.SMEM),
            pl.BlockSpec((2 * tokens // BLOCK, MIXED, BLOCK), lambda i: (last - i, 0, 0)),
            rows(width), rows(width), rows(width),
            pl.BlockSpec((GROUP, width), lambda i: (jnp.maximum((last - i) * per - 1, 0), 0)),
            rows(width), rows(width), rows(8), whole_spec(w_xt.shape), whole_spec(table.shape), ANY, ANY,
        ],
        out_specs=[whole_spec(shape.shape) for shape in shapes],
        out_shape=shapes,
        scratch_shapes=[
            pltpu.VMEM((2 * tokens + 8, width), F32),
            pltpu.VMEM((CONV - 1, 2 * tokens + 8, width), F32),
            pltpu.VMEM(w_rows.shape, BF16),
            pltpu.VMEM(lowered.shape, BF16),
            pltpu.VMEM((count, width), BF16),
            pltpu.VMEM((1, model), F32),
            pltpu.SemaphoreType.DMA((2,)),
        ],
        compiler_params=pltpu.CompilerParams(vmem_limit_bytes=VMEM),
        cost_estimate=pl.CostEstimate(flops=1 << 33, bytes_accessed=32 << 20, transcendentals=0),
        name="tail",
    )(where, mixed, d_act, conv_out, conv_in, conv_in, act, d_gate, mask, w_xt, table, w_rows, lowered)
    return list(out[:4]), out[4:8], *out[8:]


def line_ring(seqs):
    return [(i, (i + 2) % seqs) for i in range(seqs)]


def pair_swap(size, bit):
    return [(i, i ^ bit) for i in range(size)]


def gather_all(part, owned, owner, early, middle):
    seqs, shards = lax.axis_size("seq"), lax.axis_size("fsdp")
    if (seqs, shards) != (8, 4):
        whole = lax.all_gather(part, "seq", axis=0)
        owned = lax.dynamic_index_in_dim(lax.all_gather(owned, "fsdp"), owner, 0, False)
        return [whole[k] for k in range(seqs)], jnp.arange(seqs, dtype=jnp.int32), lambda *_: owned
    place, here = lax.axis_index("seq"), lax.axis_index("fsdp")
    row, column = place // 2, place % 2
    swap, ring = pair_swap(seqs, 1), line_ring(seqs)
    first, second = [], []
    for s in range(seqs):
        own = s * shards // seqs
        first.append((s * shards + own, s * shards + (own ^ 2)))
        second.append((s * shards + own, s * shards + (own ^ 1)))
        second.append((s * shards + (own ^ 2), s * shards + (own ^ 3)))
    pieces, slots = [], []
    for k in range(4):
        slot = (row - k + 4) % 4 * 2
        swapped = lax.ppermute(part, "seq", swap)
        pieces += [part, swapped]
        slots += [slot + column, slot + 1 - column]
        if k == 3:
            break
        others = (early, middle, ())[k]
        part = after(lax.ppermute(part, "seq", ring), swapped, *others)
    across = lax.ppermute(after(owned, pieces[-2]), ("seq", "fsdp"), first)

    def rest(early, late):
        same_core = jnp.where(here == owner, owned, after(across, early))
        last = lax.ppermute(same_core, ("seq", "fsdp"), second)
        return jnp.where((here ^ owner) % 2 == 0, same_core, after(last, late))

    return pieces, jnp.stack(slots).astype(jnp.int32), rest


def sum_over_seq(part):
    seqs = lax.axis_size("seq")
    shares = part.reshape((seqs, part.shape[0] // seqs) + part.shape[1:])
    shares = lax.all_to_all(shares, "seq", split_axis=0, concat_axis=0, tiled=True)
    total = jnp.sum(shares.astype(F32), axis=0).astype(BF16)
    copies = jnp.broadcast_to(total, shares.shape)
    return lax.all_to_all(copies, "seq", split_axis=0, concat_axis=0, tiled=True).reshape(part.shape), total


def scatter_shards(blocks, kind=BF16):
    shards = lax.axis_size("fsdp")
    blocks = blocks if isinstance(blocks, list) else [blocks]

    def block(j):
        parts = [lax.dynamic_index_in_dim(each, j, 0, False).astype(kind) for each in blocks]
        return jnp.concatenate(parts, axis=-2) if len(parts) > 1 else parts[0]

    if shards != 4 or lax.axis_size("seq") != 8:
        return [lax.psum_scatter(jnp.stack([block(j) for j in range(shards)]), "fsdp", scatter_dimension=0)]
    here = lax.axis_index("fsdp")
    return [block(here)] + [lax.ppermute(block(here ^ j), "fsdp", pair_swap(shards, j)) for j in range(1, shards)]


def add_up(parts):
    return sum(part.astype(F32) for part in parts)


def local(
    x_in, cotangent, doc_lengths, norm_gain, in_weight, conv_weight, conv_bias,
    x_weight, dt_weight, dt_bias, a_log, skip_weight, out_weight,
):
    seqs, shards = lax.axis_size("seq"), lax.axis_size("fsdp")
    place = lax.axis_index("seq")
    width = INNER // seqs
    tokens, model = x_in.shape[1:]
    count = tokens * seqs
    deep = model // shards

    held = INNER // shards
    owner, offset = place * width // held, place * width % held
    lanes = min(2 * width, deep)
    small = jnp.concatenate(
        [
            dt_weight.T, a_log.T, conv_weight.T, conv_bias[None], dt_bias[None], skip_weight[None],
            jnp.zeros((MIXED - DT_RANK - STATE - CONV - 3, held), BF16),
        ],
        axis=0,
    )
    small = jnp.concatenate(
        [lax.dynamic_slice_in_dim(x_weight.T, offset, width, 1), lax.dynamic_slice_in_dim(small, offset, width, 1)], axis=1
    )
    gain_rows = norm_gain.reshape(-1, lanes)
    gain_rows = jnp.pad(gain_rows, ((0, GROUP - gain_rows.shape[0]), (0, 2 * width - lanes)))
    in_cols = jnp.concatenate(
        [
            lax.dynamic_slice_in_dim(in_weight, place * width, width, 1),
            lax.dynamic_slice_in_dim(in_weight, INNER + place * width, width, 1),
        ],
        axis=1,
    )
    shard = jnp.concatenate([in_cols, gain_rows, small], axis=0)
    mask = doc_masks(doc_lengths[0], count)
    own, offsets = owns()
    rows = model // (seqs * shards)
    out_rows = lax.dynamic_slice_in_dim(out_weight, offset, width, 0)
    w_pieces = lax.all_gather(shard, "fsdp", axis=0)
    pieces, slots, w_out_of = gather_all(x_in[0], out_rows, owner, (shard, out_rows), (own, offsets, mask))
    small = lax.dynamic_index_in_dim(w_pieces[:, deep + GROUP :], owner, 0, False)
    w_xt, w_dtt, table = small[:, :width], small[:DT_RANK, width:], small[DT_RANK:, width:].astype(F32)
    cot_all = lax.all_gather(after(cotangent[0], pieces[-4]), "seq", axis=0, tiled=True)

    w_rows, gain = assemble(w_pieces, deep)
    lowered, conv_in, conv_out, act, gate, mixed = project(pieces, slots, w_rows, gain, w_xt, table, mask)
    mixed, share = sum_over_seq(mixed)
    branch, y_total, states = scan_forward(mixed, act, gate, mask, w_dtt, table, own)
    w_out = w_out_of(share, branch)
    block_part = dot_nn(branch, w_out).astype(BF16)
    block_sum = lax.psum_scatter(block_part, "seq", scatter_dimension=0, tiled=True)
    block_out = (x_in[0].astype(F32) + block_sum.astype(F32)).astype(BF16)

    d_branch = dot_nt(cot_all, w_out)

    def shared(part, *more):
        blocks = [part.reshape(seqs, shards, rows, width), *more]
        return scatter_shards([block.transpose(1, 0, 2, 3) for block in blocks])

    def spread(part):
        part = lax.all_to_all(part, "seq", split_axis=0, concat_axis=0, tiled=True)
        return part.transpose(1, 0, 2).reshape(rows, INNER).astype(F32)

    d_gate = (d_branch * y_total * silu_slope(gate)).astype(BF16)
    gate_got = shared(dot_tn(lowered, d_gate).astype(BF16))
    d_mixed, d_act, sums, dt_grad = scan_backward(
        mixed, act, gate, d_branch, mask, states, w_dtt, table, own, offsets, block_part, gate_got[0]
    )
    d_mixed, share = sum_over_seq(after(d_mixed, *gate_got[1:]))
    out_part = dot_tn(after(branch, share), cot_all).astype(BF16)
    out_sum = lax.psum_scatter(out_part.reshape(shards, width // shards, model), "fsdp", scatter_dimension=0)
    out_grad = out_sum.astype(F32)
    gate_sum = add_up([after(gate_got[0], share), *gate_got[1:]]).astype(BF16)
    d_mixed = after(d_mixed, block_sum, gate_sum, out_part)
    gate_grad = spread(gate_sum)
    if seqs == 8:
        row, column = place // 2, place % 2
        swap, ring = pair_swap(seqs, 1), line_ring(seqs)
        mine, theirs, conv_part, x_proj_grad, conv_sums = tail(
            jnp.stack([row, column]).astype(jnp.int32),
            d_mixed, d_act, conv_out, conv_in, act, d_gate, mask, w_xt, table, w_rows, lowered, seqs, shards,
        )
        small = jnp.concatenate([x_proj_grad, dt_grad, sums, conv_sums], axis=0)
        swapped = [lax.ppermute(block, "seq", swap) for block in theirs]
        conv_sum = lax.psum_scatter(conv_part, "fsdp", scatter_dimension=0)
        conv_sum = lax.all_to_all(conv_sum, "seq", split_axis=0, concat_axis=0, tiled=True)
        total = mine[1].astype(F32) + swapped[1].astype(F32)
        befores = ((), (gate_grad, out_sum), ())
        for k in range(3):
            total = after(total.astype(BF16), *befores[k])
            if k == 1:
                small = after(small, total)
            n = (k + 2) % 4
            arrived = lax.ppermute(total, "seq", ring).astype(F32)
            if k == 2:
                mine[n] = after(mine[n], conv_sum)
            total = arrived + mine[n].astype(F32) + swapped[n].astype(F32)
        d_low_own = total
    else:
        d_proj, x_proj_grad, conv_sums = finish(d_mixed, d_act, conv_out, conv_in, act, d_gate, mask, w_xt, table)
        small = jnp.concatenate([x_proj_grad, dt_grad, sums, conv_sums], axis=0)
        d_lowered = dot_nt(d_proj, w_rows)
        gain_part = jnp.sum(d_lowered * lowered.astype(F32), axis=0).reshape(seqs, 1, 1, shards * rows)
        gain_part = jnp.broadcast_to(gain_part, (seqs, shards, 8, shards * rows))
        gain_part = jnp.pad(gain_part, ((0, 0), (0, 0), (0, 0), (0, width - shards * rows)))
        conv_sum = add_up(shared(dot_tn(lowered, d_proj[:, :width]), gain_part)).astype(BF16)
        conv_sum = lax.all_to_all(conv_sum, "seq", split_axis=0, concat_axis=0, tiled=True)
        d_low_own = lax.psum_scatter(d_lowered.astype(BF16), "seq", scatter_dimension=0, tiled=True).astype(F32)
    x_own = x_in[0].astype(F32)
    inv_own = lax.rsqrt(jnp.mean(x_own * x_own, axis=1, keepdims=True) + NORM_EPS)
    normed_own = x_own * inv_own
    d_norm = d_low_own * gain
    x_grad = cotangent[0].astype(F32) + inv_own * (
        d_norm - normed_own * jnp.mean(d_norm * normed_own, axis=1, keepdims=True)
    )
    small = small.reshape(-1, shards, width // shards).transpose(1, 0, 2)
    small = lax.psum_scatter(small, "fsdp", scatter_dimension=0)
    conv_sum = conv_sum.astype(F32)
    conv_grad = conv_sum[:, :rows].transpose(1, 0, 2).reshape(rows, INNER)
    in_grad = jnp.concatenate([conv_grad, gate_grad], axis=1)
    gain_own = lax.dynamic_slice_in_dim(gain[0], (place * shards + lax.axis_index("fsdp")) * rows, rows, 0)
    gain_sum = jnp.sum(conv_sum[:, rows], axis=0)
    gain_grad = lax.dynamic_slice_in_dim(gain_sum, lax.axis_index("fsdp") * rows, rows, 0) / gain_own
    at = MIXED + DT_RANK
    end = at + 24
    return (
        block_out[None],
        x_grad[None],
        gain_grad,
        in_grad,
        small[end : end + CONV].T,
        small[end + CONV],
        small[:MIXED].T,
        small[MIXED:at].T,
        small[at + STATE + 1],
        small[at : at + STATE].T,
        small[at + STATE],
        out_grad,
    )


def solution(mesh):
    by_row, by_vec = P("fsdp", None), P("fsdp")
    tok = P("fsdp", "seq", None)
    out_row, out_vec = P(("seq", "fsdp"), None), P(("seq", "fsdp"))
    in_specs = (
        tok, tok, by_row, by_vec, by_row, by_row, by_vec, by_row, by_row, by_vec, by_row, by_vec, by_row,
    )
    out_specs = (
        tok, tok, out_vec, out_row, out_row, out_vec, out_row, out_row, out_vec, out_row, out_vec, out_row,
    )
    return jax.shard_map(local, mesh=mesh, in_specs=in_specs, out_specs=out_specs, check_vma=False)
```

```python
import jax
import jax.numpy as jnp
from jax import lax
from jax.experimental import pallas as pl
from jax.experimental.pallas import tpu as pltpu
from jax.sharding import PartitionSpec as P

INNER = 4096
STATE = 16
DT_RANK = 128
CONV = 4
MIXED = DT_RANK + 2 * STATE
NORM_EPS = 1e-05
LOG2E = 1.4426950408889634
BLOCK = 128
WIDE = 256
GROUP = 16
RESET = 1e30
VMEM = 56 << 20
F32, BF16 = jnp.float32, jnp.bfloat16


def dot_nn(a, b):
    return lax.dot_general(a, b, (((1,), (0,)), ((), ())), preferred_element_type=F32)


def dot_tn(a, b):
    return lax.dot_general(a, b, (((0,), (0,)), ((), ())), preferred_element_type=F32)


def dot_nt(a, b):
    return lax.dot_general(a, b, (((1,), (1,)), ((), ())), preferred_element_type=F32)


def silu_slope(values):
    sig = jax.nn.sigmoid(values)
    return sig * (1.0 + values * (1.0 - sig))


def softplus(values):
    return jnp.maximum(values, 0.0) + jnp.log1p(jnp.exp(-jnp.abs(values)))


def sigmoid(values):
    return 1.0 / (1.0 + jnp.exp(-values))


ANY = pl.BlockSpec(memory_space=pl.ANY)


def ordered_kernel(*refs):
    pass


def after(value, *others):
    return pl.pallas_call(
        ordered_kernel,
        in_specs=[ANY] * (1 + len(others)),
        out_specs=ANY,
        out_shape=jax.ShapeDtypeStruct(value.shape, value.dtype),
        input_output_aliases={0: 0},
        name="after",
    )(value, *others)


def doc_masks(lengths, count):
    docs = lengths.shape[0]
    order = jnp.arange(docs, dtype=jnp.int32)
    starts = jnp.sum(jnp.where(order[None, :] < order[:, None], lengths[None, :], 0), axis=1)
    places = jnp.arange(count, dtype=jnp.int32)

    def segment_of(at):
        return jnp.sum((starts[None, :] <= at[:, None]).astype(jnp.int32), axis=1)

    own = segment_of(places)
    columns = []
    for k in range(CONV):
        source = places - (CONV - 1 - k)
        columns.append(((source >= 0) & (segment_of(source) == own)).astype(F32))
    columns.append(jnp.any(starts[None, :] == places[:, None], axis=1).astype(F32))
    columns += [jnp.zeros_like(columns[0])] * (8 - len(columns))
    return jnp.stack(columns, axis=1)


ROW_LOG, ROW_CONV, ROW_CONV_B, ROW_DT_B, ROW_SKIP = 0, 16, 20, 21, 22


def assemble_kernel(pieces_ref, w_ref, gain_ref, gains_ref, w_sem, gain_sem):
    n = pieces_ref.shape[0]
    deep = w_ref.shape[0] // n
    copies = []
    for k in range(n):
        piece = pieces_ref.at[k]
        copies.append(pltpu.make_async_copy(piece.at[:deep], w_ref.at[k * deep : (k + 1) * deep], w_sem.at[k]))
        copies.append(pltpu.make_async_copy(piece.at[deep : deep + GROUP], gains_ref.at[k], gain_sem.at[k]))
    for copy in copies:
        copy.start()
    for copy in copies:
        copy.wait()
    parts = []
    for i in range(n):
        gains = gains_ref[i].astype(F32)
        lanes = min(deep, gains.shape[1])
        parts += [gains[r : r + 1, :lanes] for r in range(deep // lanes)]
    gain_ref[...] = jnp.concatenate(parts, axis=1)


def assemble(pieces, deep):
    n, _, columns = pieces.shape
    return pl.pallas_call(
        assemble_kernel,
        in_specs=[ANY],
        out_specs=[pl.BlockSpec(memory_space=pltpu.VMEM)] * 2,
        out_shape=[jax.ShapeDtypeStruct((n * deep, columns), BF16), jax.ShapeDtypeStruct((1, n * deep), F32)],
        scratch_shapes=[
            pltpu.VMEM((n, GROUP, columns), BF16),
            pltpu.SemaphoreType.DMA((n,)),
            pltpu.SemaphoreType.DMA((n,)),
        ],
        compiler_params=pltpu.CompilerParams(vmem_limit_bytes=VMEM),
        name="assemble",
    )(pieces)


def project_kernel(slots_ref, w_in_ref, gain_ref, w_xt_ref, table_ref, mask_ref, *refs):
    n = slots_ref.shape[0]
    pieces = refs[:n]
    (lowered_ref, conv_in_ref, conv_out_ref, act_ref, gate_ref, mixed_ref, line_ref, x_ref, x_sem) = refs[n:]
    rows, width = conv_in_ref.shape
    block = pl.program_id(0)
    tokens = pieces[0].shape[0]

    @pl.when(block == 0)
    def _():
        for k, piece in enumerate(pieces):
            slot = slots_ref[k]
            pltpu.make_async_copy(piece, x_ref.at[slot], x_sem.at[slot]).start()
        line_ref[:8] = jnp.zeros((8, width), F32)

    @pl.when(block > 0)
    def _():
        line_ref[:8] = line_ref[rows:]

    per = rows // tokens
    for i in range(per):
        slot = block * per + i
        pltpu.make_async_copy(pieces[0], x_ref.at[slot], x_sem.at[slot]).wait()
    x = jnp.concatenate([x_ref[block * per + i] for i in range(per)], axis=0).astype(F32)
    inv = lax.rsqrt(jnp.mean(x * x, axis=1, keepdims=True) + NORM_EPS)
    lowered_ref[...] = (x * inv * gain_ref[...]).astype(BF16)
    projected = dot_nn(lowered_ref[...], w_in_ref[...])
    conv_in = projected[:, :width].astype(BF16)
    gate_ref[...] = projected[:, width:]
    conv_in_ref[...] = conv_in
    line_ref[8:] = conv_in.astype(F32)
    conv_out = table_ref[ROW_CONV_B : ROW_CONV_B + 1, :]
    for k in range(CONV):
        taps = table_ref[ROW_CONV + k : ROW_CONV + k + 1, :]
        conv_out = conv_out + taps * line_ref[5 + k : 5 + k + rows] * mask_ref[:, k : k + 1]
    conv_out_ref[...] = conv_out
    act = (conv_out * sigmoid(conv_out)).astype(BF16)
    act_ref[...] = act
    mixed = dot_nt(w_xt_ref[...], act).astype(BF16)
    for i in range(rows // BLOCK):
        mixed_ref[i] = mixed[:, i * BLOCK : (i + 1) * BLOCK]


def rows_spec(width, index=lambda i: i, rows=BLOCK):
    return pl.BlockSpec((rows, width), lambda i: (index(i), 0))


def whole_spec(shape):
    return pl.BlockSpec(shape, lambda i: (0,) * len(shape))


def project(pieces, slots, w_rows, gain, w_xt, table, mask):
    tokens, model = pieces[0].shape
    count = tokens * len(pieces)
    width = w_xt.shape[1]

    def rows(columns):
        return rows_spec(columns, rows=WIDE)

    return pl.pallas_call(
        project_kernel,
        grid=(count // WIDE,),
        in_specs=[
            pl.BlockSpec(memory_space=pltpu.SMEM), whole_spec(w_rows.shape), whole_spec(gain.shape),
            whole_spec(w_xt.shape), whole_spec(table.shape), rows(8), *[ANY] * len(pieces),
        ],
        out_specs=[
            rows(model), rows(width), rows(width), rows(width), rows(width),
            pl.BlockSpec((WIDE // BLOCK, MIXED, BLOCK), lambda i: (i, 0, 0)),
        ],
        out_shape=[
            jax.ShapeDtypeStruct((count, model), BF16),
            jax.ShapeDtypeStruct((count, width), BF16),
            jax.ShapeDtypeStruct((count, width), F32),
            jax.ShapeDtypeStruct((count, width), BF16),
            jax.ShapeDtypeStruct((count, width), F32),
            jax.ShapeDtypeStruct((count // BLOCK, MIXED, BLOCK), BF16),
        ],
        scratch_shapes=[
            pltpu.VMEM((WIDE + 8, width), F32),
            pltpu.VMEM((len(pieces), tokens, model), BF16),
            pltpu.SemaphoreType.DMA((len(pieces),)),
        ],
        compiler_params=pltpu.CompilerParams(vmem_limit_bytes=VMEM),
        cost_estimate=pl.CostEstimate(flops=2 * count * model * 2 * width, bytes_accessed=20 << 20, transcendentals=0),
        name="project",
    )(slots, w_rows, gain, w_xt, table, mask, *pieces)


def spread_groups(values):
    state = lax.broadcasted_iota(jnp.int32, (STATE, GROUP * STATE), 0)
    column = lax.broadcasted_iota(jnp.int32, (STATE, GROUP * STATE), 1)
    pick = jnp.where((column & (STATE - 1)) == state, 1.0, 0.0).astype(BF16)
    tiled = dot_tn(values, pick)
    token = lax.broadcasted_iota(jnp.int32, (BLOCK, GROUP * STATE), 0)
    column = lax.broadcasted_iota(jnp.int32, (BLOCK, GROUP * STATE), 1)
    return jnp.where((token & (GROUP - 1)) == (column >> 4), tiled, 0.0).astype(BF16)


def spread_lanes(values, own_ref, out_ref):
    ones = jnp.ones((BLOCK, BLOCK), BF16)
    for g in range(BLOCK // GROUP):
        here = slice(g * GROUP * STATE, (g + 1) * GROUP * STATE)
        out_ref[here] = dot_nn(jnp.concatenate([values] * GROUP, axis=0) * own_ref[here], ones)


def wide(values, width):
    lanes = values.shape[1]
    return values[:, :width] if width < lanes else jnp.concatenate([values] * (width // lanes), axis=1)


def owns():
    row, column = (lax.broadcasted_iota(jnp.int32, (BLOCK * STATE, BLOCK), i) for i in (0, 1))
    ahead = column - row // STATE
    return (ahead == 0).astype(BF16), ahead[: GROUP * STATE]


def forward_kernel(mixed_ref, act_ref, gate_ref, mask_ref, w_dtt_ref, table_ref, own_ref,
                   branch_ref, y_ref, states_ref, h_ref, stepd_ref, drive_ref, b_ref):
    @pl.when(pl.program_id(0) == 0)
    def _():
        h_ref[...] = jnp.zeros_like(h_ref)

    width = act_ref.shape[1]
    act = act_ref[...].astype(F32)
    pre = dot_tn(mixed_ref[0, :DT_RANK], w_dtt_ref[...]) + table_ref[ROW_DT_B : ROW_DT_B + 1, :]
    step = softplus(pre)
    stepd_ref[...] = jnp.where(mask_ref[:, CONV : CONV + 1] > 0.0, RESET, step)
    drive_ref[...] = step * act
    spread_lanes(mixed_ref[0, DT_RANK : DT_RANK + STATE], own_ref, b_ref)
    rate = -jnp.exp(table_ref[ROW_LOG : ROW_LOG + STATE, :]) * LOG2E

    def group(g, h):
        r0 = pl.multiple_of(g * GROUP, GROUP)
        stepd = stepd_ref[pl.ds(r0, GROUP), :]
        drive = drive_ref[pl.ds(r0, GROUP), :]
        for j in range(GROUP):
            at = pl.multiple_of((r0 + j) * STATE, STATE)
            b = wide(b_ref[pl.ds(at, STATE), :], width)
            h = jnp.exp2(stepd[j : j + 1, :] * rate) * h + drive[j : j + 1, :] * b
            states_ref[pl.ds(at, STATE), :] = h.astype(BF16)
        return h

    h_ref[...] = lax.fori_loop(0, BLOCK // GROUP, group, h_ref[...])
    c = spread_groups(mixed_ref[0, DT_RANK + STATE :])
    for g in range(BLOCK // GROUP):
        at = g * GROUP
        y_ref[at : at + GROUP, :] = dot_nn(c[at : at + GROUP], states_ref[at * STATE : (at + GROUP) * STATE])
    y_total = y_ref[...] + table_ref[ROW_SKIP : ROW_SKIP + 1, :] * act
    y_ref[...] = y_total
    gate = gate_ref[...]
    branch_ref[...] = (y_total * (gate * sigmoid(gate))).astype(BF16)


def scan_forward(mixed, act, gate, mask, w_dtt, table, own):
    count, width = act.shape
    return pl.pallas_call(
        forward_kernel,
        grid=(count // BLOCK,),
        in_specs=[
            pl.BlockSpec((1, MIXED, BLOCK), lambda i: (i, 0, 0)), rows_spec(width), rows_spec(width), rows_spec(8),
            whole_spec(w_dtt.shape), whole_spec(table.shape), whole_spec(own.shape),
        ],
        out_specs=[rows_spec(width), rows_spec(width), pl.BlockSpec((BLOCK * STATE, width), lambda i: (i, 0))],
        out_shape=[
            jax.ShapeDtypeStruct((count, width), BF16),
            jax.ShapeDtypeStruct((count, width), F32),
            jax.ShapeDtypeStruct((count * STATE, width), BF16),
        ],
        scratch_shapes=[
            pltpu.VMEM((STATE, width), F32),
            pltpu.VMEM((BLOCK, width), F32),
            pltpu.VMEM((BLOCK, width), F32),
            pltpu.VMEM((BLOCK * STATE, BLOCK), F32),
        ],
        compiler_params=pltpu.CompilerParams(vmem_limit_bytes=VMEM),
        cost_estimate=pl.CostEstimate(flops=8 * count * width * STATE * 16, bytes_accessed=64 << 20, transcendentals=0),
        name="scan_forward",
    )(mixed, act, gate, mask, w_dtt, table, own)


def backward_kernel(mixed_ref, act_ref, gate_ref, d_branch_ref, mask_ref, states_ref, ahead_ref,
                    w_dtt_ref, table_ref, own_ref, offset_ref, _block, _gate,
                    d_mixed_ref, d_act_ref, sums_ref, dt_grad_ref,
                    p_ref, dy_ref, stepd_ref, c_ref, s1_ref, s2_ref, bg_ref, dyt_ref, sat_ref, d_b_ref, d_c_ref,
                    adj_a_ref, adj_b_ref, rq_a_ref, rq_b_ref):
    first = pl.program_id(0) == 0
    width = act_ref.shape[1]

    @pl.when(first)
    def _():
        p_ref[...] = jnp.zeros_like(p_ref)
        sums_ref[...] = jnp.zeros_like(sums_ref)
        dt_grad_ref[...] = jnp.zeros_like(dt_grad_ref)
        adj_b_ref[...] = jnp.zeros_like(adj_b_ref)
        rq_b_ref[...] = jnp.zeros_like(rq_b_ref)
        d_b_ref[...] = jnp.zeros_like(d_b_ref)
        d_c_ref[...] = jnp.zeros_like(d_c_ref)
        bg_ref[BLOCK:] = jnp.zeros((GROUP, GROUP * STATE), BF16)

    act = act_ref[...].astype(F32)
    gate = gate_ref[...]
    sig = sigmoid(gate)
    d_branch = d_branch_ref[...]
    dy = d_branch * (gate * sig)
    pre = dot_tn(mixed_ref[0, :DT_RANK], w_dtt_ref[...]) + table_ref[ROW_DT_B : ROW_DT_B + 1, :]
    step = softplus(pre)
    dy_ref[...] = dy
    stepd_ref[...] = jnp.where(mask_ref[:, CONV : CONV + 1] > 0.0, RESET, step)
    dyt_ref[...] = dy.T.astype(BF16)
    sat_ref[...] = (step * act).T.astype(BF16)
    spread_lanes(mixed_ref[0, DT_RANK + STATE :], own_ref, c_ref)
    bg_ref[:BLOCK] = spread_groups(mixed_ref[0, DT_RANK : DT_RANK + STATE])
    raw = -jnp.exp(table_ref[ROW_LOG : ROW_LOG + STATE, :])
    rate = raw * LOG2E
    groups = BLOCK // GROUP
    per = GROUP * STATE
    token = lax.broadcasted_iota(jnp.int32, (GROUP, per), 0)
    column = lax.broadcasted_iota(jnp.int32, (GROUP, per), 1)
    ones = jnp.where(token == (column >> 4), 1.0, 0.0).astype(BF16)
    pick = jnp.where(token == (column & (STATE - 1)), 1.0, 0.0).astype(BF16)

    def steps(g, p, total, adj_ref, rq_ref):
        r0 = pl.multiple_of(g * GROUP, GROUP)
        dy_g = dy_ref[pl.ds(r0, GROUP), :]
        stepd_g = stepd_ref[pl.ds(r0, GROUP), :]
        for j in reversed(range(GROUP)):
            at = pl.multiple_of((r0 + j) * STATE, STATE)
            if j:
                behind = pl.multiple_of((r0 + j - 1) * STATE, STATE)
                before = states_ref[pl.ds(behind, STATE), :]
            else:
                behind = pl.multiple_of(jnp.maximum(r0 - 1, 0) * STATE, STATE)
                before = jnp.where(g > 0, states_ref[pl.ds(behind, STATE), :], ahead_ref[...])
            adj = dy_g[j : j + 1, :] * wide(c_ref[pl.ds(at, STATE), :], width) + p
            adj_ref[j * STATE : (j + 1) * STATE] = adj.astype(BF16)
            p = jnp.exp2(stepd_g[j : j + 1, :] * rate) * adj
            rq = raw * (p * before.astype(F32))
            rq_ref[j * STATE : (j + 1) * STATE] = rq.astype(BF16)
            total = total + stepd_g[j : j + 1, :] * rq
        return p, total

    def sums(g, state_rows, adj_ref, rq_ref):
        r0 = pl.multiple_of(g * GROUP, GROUP)
        adj = adj_ref[...]
        s1_ref[pl.ds(r0, GROUP), :] = dot_nn(bg_ref[pl.ds(r0, GROUP), :], adj)
        s2_ref[pl.ds(r0, GROUP), :] = dot_nn(ones, rq_ref[...])
        here = offset_ref[...] == r0
        d_b_ref[...] = jnp.where(here, dot_nn(adj, sat_ref[...]), d_b_ref[...])
        states = states_ref[pl.ds(state_rows, per), :]
        d_c_ref[...] = jnp.where(here, dot_nn(states, dyt_ref[...]), d_c_ref[...])

    def pair(i, carry):
        p, total = carry
        high = groups - 1 - 2 * i
        low = high - 1
        rows = pl.multiple_of(jnp.minimum(low + 2, groups - 1) * per, per)
        sums(low + 2, rows, adj_b_ref, rq_b_ref)
        p, total = steps(high, p, total, adj_a_ref, rq_a_ref)
        sums(high, pl.multiple_of(high * per, per), adj_a_ref, rq_a_ref)
        return steps(low, p, total, adj_b_ref, rq_b_ref)

    p, total = lax.fori_loop(0, groups // 2, pair, (p_ref[...], sums_ref[:STATE]))
    sums(0, 0, adj_b_ref, rq_b_ref)
    p_ref[...] = p
    sums_ref[:STATE] = total
    d_mixed_ref[0, DT_RANK : DT_RANK + STATE] = dot_nn(pick, d_b_ref[...].astype(BF16)).astype(BF16)
    d_mixed_ref[0, DT_RANK + STATE :] = dot_nn(pick, d_c_ref[...].astype(BF16)).astype(BF16)

    s1, s2 = s1_ref[:BLOCK], s2_ref[:BLOCK]
    d_act_ref[...] = dy * table_ref[ROW_SKIP : ROW_SKIP + 1, :] + step * s1
    d_pre = (act * s1 + s2) * jnp.exp(pre - step)
    sums_ref[STATE : STATE + 1] += jnp.sum(dy * act, axis=0, keepdims=True)
    sums_ref[STATE + 1 : STATE + 2] += jnp.sum(d_pre, axis=0, keepdims=True)
    d_pre = d_pre.astype(BF16)
    dt_grad_ref[...] += dot_nn(mixed_ref[0, :DT_RANK], d_pre)
    d_mixed_ref[0, :DT_RANK] = dot_nt(w_dtt_ref[...], d_pre).astype(BF16)


def scan_backward(mixed, act, gate, d_branch, mask, states, w_dtt, table, own, offsets, *before):
    count, width = act.shape
    blocks = count // BLOCK
    last = blocks - 1
    rows = rows_spec(width, lambda i: last - i)
    mixed_spec = pl.BlockSpec((1, MIXED, BLOCK), lambda i: (last - i, 0, 0))
    per = GROUP * STATE
    return pl.pallas_call(
        backward_kernel,
        grid=(blocks,),
        in_specs=[
            mixed_spec, rows, rows, rows, rows_spec(8, lambda i: last - i),
            pl.BlockSpec((BLOCK * STATE, width), lambda i: (last - i, 0)),
            pl.BlockSpec((STATE, width), lambda i: (jnp.maximum((last - i) * BLOCK - 1, 0), 0)),
            whole_spec(w_dtt.shape), whole_spec(table.shape), whole_spec(own.shape), whole_spec(offsets.shape), ANY, ANY,
        ],
        out_specs=[mixed_spec, rows, whole_spec((24, width)), whole_spec((DT_RANK, width))],
        out_shape=[
            jax.ShapeDtypeStruct((blocks, MIXED, BLOCK), BF16),
            jax.ShapeDtypeStruct((count, width), F32),
            jax.ShapeDtypeStruct((24, width), F32),
            jax.ShapeDtypeStruct((DT_RANK, width), F32),
        ],
        scratch_shapes=[
            pltpu.VMEM((STATE, width), F32),
            pltpu.VMEM((BLOCK, width), F32),
            pltpu.VMEM((BLOCK, width), F32),
            pltpu.VMEM((BLOCK * STATE, BLOCK), F32),
            pltpu.VMEM((BLOCK + GROUP, width), F32),
            pltpu.VMEM((BLOCK + GROUP, width), F32),
            pltpu.VMEM((BLOCK + GROUP, per), BF16),
            pltpu.VMEM((width, BLOCK), BF16),
            pltpu.VMEM((width, BLOCK), BF16),
            pltpu.VMEM((per, BLOCK), F32),
            pltpu.VMEM((per, BLOCK), F32),
            pltpu.VMEM((per, width), BF16),
            pltpu.VMEM((per, width), BF16),
            pltpu.VMEM((per, width), BF16),
            pltpu.VMEM((per, width), BF16),
        ],
        compiler_params=pltpu.CompilerParams(vmem_limit_bytes=VMEM),
        cost_estimate=pl.CostEstimate(flops=8 * count * width * STATE * 32, bytes_accessed=96 << 20, transcendentals=0),
        name="scan_backward",
    )(mixed, act, gate, d_branch, mask, states, states, w_dtt, table, own, offsets, *before)


def finish_kernel(mixed_ref, d_act_ref, conv_out_ref, conv_in_ref, ahead_ref, act_ref, d_gate_ref, mask_ref, w_xt_ref,
                  table_ref, d_proj_ref, x_grad_ref, sums_ref, line_ref, masked_ref):
    rows, width = act_ref.shape
    d_conv_in = conv_backward(
        (mixed_ref, d_act_ref, conv_out_ref, conv_in_ref, ahead_ref, act_ref, mask_ref, w_xt_ref, table_ref,
         x_grad_ref, sums_ref, line_ref, masked_ref), rows, width, pl.program_id(0) == 0
    )
    d_proj_ref[:, :width] = d_conv_in.astype(BF16)
    d_proj_ref[:, width:] = d_gate_ref[...]


def finish(mixed, d_act, conv_out, conv_in, act, d_gate, mask, w_xt, table):
    count, width = act.shape
    blocks = count // WIDE
    last = blocks - 1

    def rows(columns):
        return rows_spec(columns, lambda i: last - i, WIDE)

    per = WIDE // GROUP
    return pl.pallas_call(
        finish_kernel,
        grid=(blocks,),
        in_specs=[
            pl.BlockSpec((WIDE // BLOCK, MIXED, BLOCK), lambda i: (last - i, 0, 0)), rows(width), rows(width), rows(width),
            pl.BlockSpec((GROUP, width), lambda i: (jnp.maximum((last - i) * per - 1, 0), 0)),
            rows(width), rows(width), rows(8), whole_spec(w_xt.shape), whole_spec(table.shape),
        ],
        out_specs=[rows(2 * width), whole_spec((MIXED, width)), whole_spec((8, width))],
        out_shape=[
            jax.ShapeDtypeStruct((count, 2 * width), BF16),
            jax.ShapeDtypeStruct((MIXED, width), F32),
            jax.ShapeDtypeStruct((8, width), F32),
        ],
        scratch_shapes=[pltpu.VMEM((WIDE + 8, width), F32), pltpu.VMEM((CONV - 1, WIDE + 8, width), F32)],
        compiler_params=pltpu.CompilerParams(vmem_limit_bytes=VMEM),
        cost_estimate=pl.CostEstimate(flops=1 << 31, bytes_accessed=12 << 20, transcendentals=0),
        name="finish",
    )(mixed, d_act, conv_out, conv_in, conv_in, act, d_gate, mask, w_xt, table)


def conv_backward(refs, rows, width, first):
    (mixed_ref, d_act_ref, conv_out_ref, conv_in_ref, ahead_ref, act_ref, mask_ref, w_xt_ref, table_ref,
     x_grad_ref, sums_ref, line_ref, masked_ref) = refs

    @pl.when(first)
    def _():
        x_grad_ref[...] = jnp.zeros_like(x_grad_ref)
        sums_ref[...] = jnp.zeros_like(sums_ref)
        for k in range(CONV - 1):
            masked_ref[k, rows:] = jnp.zeros((8, width), F32)

    @pl.when(jnp.logical_not(first))
    def _():
        for k in range(CONV - 1):
            masked_ref[k, rows:] = masked_ref[k, :8]

    mixed = jnp.concatenate([mixed_ref[i] for i in range(rows // BLOCK)], axis=1)
    x_grad_ref[...] += dot_nn(mixed, act_ref[...])
    d_act = d_act_ref[...] + dot_tn(mixed, w_xt_ref[...])
    conv_out = conv_out_ref[...]
    sig = sigmoid(conv_out)
    d_conv = d_act * (sig * (1.0 + conv_out * (1.0 - sig)))
    sums_ref[CONV : CONV + 1] += jnp.sum(d_conv, axis=0, keepdims=True)
    line_ref[:8] = ahead_ref[...].astype(F32)[8:]
    line_ref[8:] = conv_in_ref[...].astype(F32)
    d_conv_in = jnp.zeros((rows, width), F32)
    for k in range(CONV):
        masked = d_conv * mask_ref[:, k : k + 1]
        sums_ref[k : k + 1] += jnp.sum(masked * line_ref[5 + k : 5 + k + rows], axis=0, keepdims=True)
        if k < CONV - 1:
            masked_ref[k, :rows] = masked
            masked = masked_ref[k, CONV - 1 - k : CONV - 1 - k + rows]
        d_conv_in = d_conv_in + table_ref[ROW_CONV + k : ROW_CONV + k + 1, :] * masked
    return d_conv_in


def tail_kernel(where_ref, mixed_ref, d_act_ref, conv_out_ref, conv_in_ref, ahead_ref, act_ref, d_gate_ref, mask_ref,
                w_xt_ref, table_ref, w_any, lowered_any, *refs):
    mine, theirs, part_ref = refs[:4], refs[4:8], refs[8]
    (x_grad_ref, sums_ref, line_ref, masked_ref, w_ref, lowered_ref, d_conv_ref, gain_ref,
     sem_ref) = refs[9:]
    step = pl.program_id(0)
    rows, width = act_ref.shape
    tokens, model = mine[0].shape
    row, column = where_ref[0], where_ref[1]
    block = pl.num_programs(0) - 1 - step
    w_copy = pltpu.make_async_copy(w_any, w_ref, sem_ref.at[0])
    lowered_copy = pltpu.make_async_copy(lowered_any, lowered_ref, sem_ref.at[1])

    @pl.when(step == 0)
    def _():
        w_copy.start()
        lowered_copy.start()
        gain_ref[...] = jnp.zeros_like(gain_ref)

    d_conv_in = conv_backward(
        (mixed_ref, d_act_ref, conv_out_ref, conv_in_ref, ahead_ref, act_ref, mask_ref, w_xt_ref, table_ref,
         x_grad_ref, sums_ref, line_ref, masked_ref), rows, width, step == 0
    ).astype(BF16)
    at = pl.multiple_of(block * rows, rows)
    d_conv_ref[pl.ds(at, rows), :] = d_conv_in

    @pl.when(step == 0)
    def _():
        w_copy.wait()
        lowered_copy.wait()

    d_proj = jnp.concatenate([d_conv_in, d_gate_ref[...]], axis=1)
    out = dot_nt(d_proj, w_ref[...])
    gain_ref[...] += jnp.sum(out * lowered_ref[pl.ds(at, rows), :].astype(F32), axis=0, keepdims=True)
    halves = out[:tokens].astype(BF16), out[tokens:].astype(BF16)
    k = lax.rem(row - block + 4, 4)
    for j in range(4):
        for c in range(2):

            @pl.when(jnp.logical_and(k == j, column == c))
            def _(j=j, c=c):
                mine[j][...] = halves[c]
                theirs[j][...] = halves[1 - c]

    @pl.when(block == 0)
    def _():
        shards, places, each, _ = part_ref.shape
        each = each - 8
        many = shards * each

        def one(s, carry):
            lanes = pl.ds(pl.multiple_of(s * many, many), many)
            chunk = dot_tn(lowered_ref[:, lanes], d_conv_ref[...]).astype(BF16)
            gains = jnp.broadcast_to(gain_ref[:, lanes], (8, many)).astype(BF16)
            for j in range(shards):
                part_ref[j, s, :each] = chunk[j * each : (j + 1) * each]
                part_ref[j, s, each:] = jnp.concatenate([gains] * (width // many), axis=1)
            return carry

        lax.fori_loop(0, places, one, 0)


def tail(where, mixed, d_act, conv_out, conv_in, act, d_gate, mask, w_xt, table, w_rows, lowered, seqs, shards):
    count, width = act.shape
    model = lowered.shape[1]
    tokens, many = count // seqs, model // seqs
    blocks = count // (2 * tokens)
    last = blocks - 1
    per = 2 * tokens // GROUP

    def rows(columns):
        return pl.BlockSpec((2 * tokens, columns), lambda i: (last - i, 0))

    shapes = [jax.ShapeDtypeStruct((tokens, model), BF16)] * 8
    shapes += [jax.ShapeDtypeStruct((shards, seqs, many // shards + 8, width), BF16)]
    shapes += [jax.ShapeDtypeStruct((MIXED, width), F32), jax.ShapeDtypeStruct((8, width), F32)]
    out = pl.pallas_call(
        tail_kernel,
        grid=(blocks,),
        in_specs=[
            pl.BlockSpec(memory_space=pltpu.SMEM),
            pl.BlockSpec((2 * tokens // BLOCK, MIXED, BLOCK), lambda i: (last - i, 0, 0)),
            rows(width), rows(width), rows(width),
            pl.BlockSpec((GROUP, width), lambda i: (jnp.maximum((last - i) * per - 1, 0), 0)),
            rows(width), rows(width), rows(8), whole_spec(w_xt.shape), whole_spec(table.shape), ANY, ANY,
        ],
        out_specs=[whole_spec(shape.shape) for shape in shapes],
        out_shape=shapes,
        scratch_shapes=[
            pltpu.VMEM((2 * tokens + 8, width), F32),
            pltpu.VMEM((CONV - 1, 2 * tokens + 8, width), F32),
            pltpu.VMEM(w_rows.shape, BF16),
            pltpu.VMEM(lowered.shape, BF16),
            pltpu.VMEM((count, width), BF16),
            pltpu.VMEM((1, model), F32),
            pltpu.SemaphoreType.DMA((2,)),
        ],
        compiler_params=pltpu.CompilerParams(vmem_limit_bytes=VMEM),
        cost_estimate=pl.CostEstimate(flops=1 << 33, bytes_accessed=32 << 20, transcendentals=0),
        name="tail",
    )(where, mixed, d_act, conv_out, conv_in, conv_in, act, d_gate, mask, w_xt, table, w_rows, lowered)
    return list(out[:4]), out[4:8], *out[8:]


def line_ring(seqs):
    return [(i, (i + 2) % seqs) for i in range(seqs)]


def pair_swap(size, bit):
    return [(i, i ^ bit) for i in range(size)]


def gather_all(part, owned, owner, early, middle):
    seqs, shards = lax.axis_size("seq"), lax.axis_size("fsdp")
    if (seqs, shards) != (8, 4):
        whole = lax.all_gather(part, "seq", axis=0)
        owned = lax.dynamic_index_in_dim(lax.all_gather(owned, "fsdp"), owner, 0, False)
        return [whole[k] for k in range(seqs)], jnp.arange(seqs, dtype=jnp.int32), lambda *_: owned
    place, here = lax.axis_index("seq"), lax.axis_index("fsdp")
    row, column = place // 2, place % 2
    swap, ring = pair_swap(seqs, 1), line_ring(seqs)
    first, second = [], []
    for s in range(seqs):
        own = s * shards // seqs
        first.append((s * shards + own, s * shards + (own ^ 2)))
        second.append((s * shards + own, s * shards + (own ^ 1)))
        second.append((s * shards + (own ^ 2), s * shards + (own ^ 3)))
    pieces, slots = [], []
    for k in range(4):
        slot = (row - k + 4) % 4 * 2
        swapped = lax.ppermute(part, "seq", swap)
        pieces += [part, swapped]
        slots += [slot + column, slot + 1 - column]
        if k == 3:
            break
        others = (early, middle, ())[k]
        part = after(lax.ppermute(part, "seq", ring), swapped, *others)
    across = lax.ppermute(after(owned, pieces[-2]), ("seq", "fsdp"), first)

    def rest(early, late):
        same_core = jnp.where(here == owner, owned, after(across, early))
        last = lax.ppermute(same_core, ("seq", "fsdp"), second)
        return jnp.where((here ^ owner) % 2 == 0, same_core, after(last, late))

    return pieces, jnp.stack(slots).astype(jnp.int32), rest


def sum_over_seq(part):
    seqs = lax.axis_size("seq")
    shares = part.reshape((seqs, part.shape[0] // seqs) + part.shape[1:])
    shares = lax.all_to_all(shares, "seq", split_axis=0, concat_axis=0, tiled=True)
    total = jnp.sum(shares.astype(F32), axis=0).astype(BF16)
    copies = jnp.broadcast_to(total, shares.shape)
    return lax.all_to_all(copies, "seq", split_axis=0, concat_axis=0, tiled=True).reshape(part.shape), total


def scatter_shards(blocks, kind=BF16):
    shards = lax.axis_size("fsdp")
    blocks = blocks if isinstance(blocks, list) else [blocks]

    def block(j):
        parts = [lax.dynamic_index_in_dim(each, j, 0, False).astype(kind) for each in blocks]
        return jnp.concatenate(parts, axis=-2) if len(parts) > 1 else parts[0]

    if shards != 4 or lax.axis_size("seq") != 8:
        return [lax.psum_scatter(jnp.stack([block(j) for j in range(shards)]), "fsdp", scatter_dimension=0)]
    here = lax.axis_index("fsdp")
    return [block(here)] + [lax.ppermute(block(here ^ j), "fsdp", pair_swap(shards, j)) for j in range(1, shards)]


def add_up(parts):
    return sum(part.astype(F32) for part in parts)


def local(
    x_in, cotangent, doc_lengths, norm_gain, in_weight, conv_weight, conv_bias,
    x_weight, dt_weight, dt_bias, a_log, skip_weight, out_weight,
):
    seqs, shards = lax.axis_size("seq"), lax.axis_size("fsdp")
    place = lax.axis_index("seq")
    width = INNER // seqs
    tokens, model = x_in.shape[1:]
    count = tokens * seqs
    deep = model // shards

    held = INNER // shards
    owner, offset = place * width // held, place * width % held
    lanes = min(2 * width, deep)
    small = jnp.concatenate(
        [
            dt_weight.T, a_log.T, conv_weight.T, jnp.stack([conv_bias, dt_bias, skip_weight]),
            jnp.zeros((MIXED - DT_RANK - STATE - CONV - 3, held), BF16),
        ],
        axis=0,
    )
    small = jnp.concatenate(
        [lax.dynamic_slice_in_dim(x_weight.T, offset, width, 1), lax.dynamic_slice_in_dim(small, offset, width, 1)], axis=1
    )
    gain_rows = norm_gain.reshape(-1, lanes)
    gain_rows = jnp.pad(gain_rows, ((0, GROUP - gain_rows.shape[0]), (0, 2 * width - lanes)))
    in_cols = jnp.concatenate(
        [
            lax.dynamic_slice_in_dim(in_weight, place * width, width, 1),
            lax.dynamic_slice_in_dim(in_weight, INNER + place * width, width, 1),
        ],
        axis=1,
    )
    shard = jnp.concatenate([in_cols, gain_rows, small], axis=0)
    mask = doc_masks(doc_lengths[0], count)
    own, offsets = owns()
    rows = model // (seqs * shards)
    out_rows = lax.dynamic_slice_in_dim(out_weight, offset, width, 0)
    w_pieces = lax.all_gather(shard, "fsdp", axis=0)
    pieces, slots, w_out_of = gather_all(x_in[0], out_rows, owner, (shard, out_rows), (own, offsets, mask))
    small = lax.dynamic_index_in_dim(w_pieces[:, deep + GROUP :], owner, 0, False)
    w_xt, w_dtt, table = small[:, :width], small[:DT_RANK, width:], small[DT_RANK:, width:].astype(F32)
    cot_all = lax.all_gather(after(cotangent[0], pieces[-4]), "seq", axis=0, tiled=True)

    w_rows, gain = assemble(w_pieces, deep)
    lowered, conv_in, conv_out, act, gate, mixed = project(pieces, slots, w_rows, gain, w_xt, table, mask)
    mixed, share = sum_over_seq(mixed)
    branch, y_total, states = scan_forward(mixed, act, gate, mask, w_dtt, table, own)
    w_out = w_out_of(share, branch)
    block_part = dot_nn(branch, w_out).astype(BF16)
    block_sum = lax.psum_scatter(block_part, "seq", scatter_dimension=0, tiled=True)
    block_out = (x_in[0].astype(F32) + block_sum.astype(F32)).astype(BF16)

    d_branch = dot_nt(cot_all, w_out)

    def shared(part, *more):
        blocks = [part.reshape(seqs, shards, rows, width), *more]
        return scatter_shards([block.transpose(1, 0, 2, 3) for block in blocks])

    def spread(part):
        part = lax.all_to_all(part, "seq", split_axis=0, concat_axis=0, tiled=True)
        return part.transpose(1, 0, 2).reshape(rows, INNER).astype(F32)

    d_gate = (d_branch * y_total * silu_slope(gate)).astype(BF16)
    gate_got = shared(dot_tn(lowered, d_gate).astype(BF16))
    d_mixed, d_act, sums, dt_grad = scan_backward(
        mixed, act, gate, d_branch, mask, states, w_dtt, table, own, offsets, block_part, gate_got[0]
    )
    d_mixed, share = sum_over_seq(after(d_mixed, *gate_got[1:]))
    out_part = dot_tn(after(branch, share), cot_all).astype(BF16)
    out_sum = lax.psum_scatter(out_part.reshape(shards, width // shards, model), "fsdp", scatter_dimension=0)
    out_grad = out_sum.astype(F32)
    gate_sum = add_up([after(gate_got[0], share), *gate_got[1:]]).astype(BF16)
    d_mixed = after(d_mixed, block_sum, gate_sum, out_part)
    gate_grad = spread(gate_sum)
    if seqs == 8:
        row, column = place // 2, place % 2
        swap, ring = pair_swap(seqs, 1), line_ring(seqs)
        mine, theirs, conv_part, x_proj_grad, conv_sums = tail(
            jnp.stack([row, column]).astype(jnp.int32),
            d_mixed, d_act, conv_out, conv_in, act, d_gate, mask, w_xt, table, w_rows, lowered, seqs, shards,
        )
        small = jnp.concatenate([x_proj_grad, dt_grad, sums, conv_sums], axis=0)
        swapped = [lax.ppermute(block, "seq", swap) for block in theirs]
        conv_sum = lax.psum_scatter(conv_part, "fsdp", scatter_dimension=0)
        conv_sum = lax.all_to_all(conv_sum, "seq", split_axis=0, concat_axis=0, tiled=True)
        total = mine[1].astype(F32) + swapped[1].astype(F32)
        befores = ((), (gate_grad, out_sum), ())
        for k in range(3):
            total = after(total.astype(BF16), *befores[k])
            if k == 1:
                small = after(small, total)
            n = (k + 2) % 4
            arrived = lax.ppermute(total, "seq", ring).astype(F32)
            if k == 2:
                mine[n] = after(mine[n], conv_sum)
            total = arrived + mine[n].astype(F32) + swapped[n].astype(F32)
        d_low_own = total
    else:
        d_proj, x_proj_grad, conv_sums = finish(d_mixed, d_act, conv_out, conv_in, act, d_gate, mask, w_xt, table)
        small = jnp.concatenate([x_proj_grad, dt_grad, sums, conv_sums], axis=0)
        d_lowered = dot_nt(d_proj, w_rows)
        gain_part = jnp.sum(d_lowered * lowered.astype(F32), axis=0).reshape(seqs, 1, 1, shards * rows)
        gain_part = jnp.broadcast_to(gain_part, (seqs, shards, 8, shards * rows))
        gain_part = jnp.pad(gain_part, ((0, 0), (0, 0), (0, 0), (0, width - shards * rows)))
        conv_sum = add_up(shared(dot_tn(lowered, d_proj[:, :width]), gain_part)).astype(BF16)
        conv_sum = lax.all_to_all(conv_sum, "seq", split_axis=0, concat_axis=0, tiled=True)
        d_low_own = lax.psum_scatter(d_lowered.astype(BF16), "seq", scatter_dimension=0, tiled=True).astype(F32)
    x_own = x_in[0].astype(F32)
    inv_own = lax.rsqrt(jnp.mean(x_own * x_own, axis=1, keepdims=True) + NORM_EPS)
    normed_own = x_own * inv_own
    d_norm = d_low_own * gain
    x_grad = cotangent[0].astype(F32) + inv_own * (
        d_norm - normed_own * jnp.mean(d_norm * normed_own, axis=1, keepdims=True)
    )
    small = small.reshape(-1, shards, width // shards).transpose(1, 0, 2)
    small = lax.psum_scatter(small, "fsdp", scatter_dimension=0)
    conv_sum = conv_sum.astype(F32)
    conv_grad = conv_sum[:, :rows].transpose(1, 0, 2).reshape(rows, INNER)
    in_grad = jnp.concatenate([conv_grad, gate_grad], axis=1)
    gain_own = lax.dynamic_slice_in_dim(gain[0], (place * shards + lax.axis_index("fsdp")) * rows, rows, 0)
    gain_sum = jnp.sum(conv_sum[:, rows], axis=0)
    gain_grad = lax.dynamic_slice_in_dim(gain_sum, lax.axis_index("fsdp") * rows, rows, 0) / gain_own
    at = MIXED + DT_RANK
    end = at + 24
    return (
        block_out[None],
        x_grad[None],
        gain_grad,
        in_grad,
        small[end : end + CONV].T,
        small[end + CONV],
        small[:MIXED].T,
        small[MIXED:at].T,
        small[at + STATE + 1],
        small[at : at + STATE].T,
        small[at + STATE],
        out_grad,
    )


def solution(mesh):
    by_row, by_vec = P("fsdp", None), P("fsdp")
    tok = P("fsdp", "seq", None)
    out_row, out_vec = P(("seq", "fsdp"), None), P(("seq", "fsdp"))
    in_specs = (
        tok, tok, by_row, by_vec, by_row, by_row, by_vec, by_row, by_row, by_vec, by_row, by_vec, by_row,
    )
    out_specs = (
        tok, tok, out_vec, out_row, out_row, out_vec, out_row, out_row, out_vec, out_row, out_vec, out_row,
    )
    return jax.shard_map(local, mesh=mesh, in_specs=in_specs, out_specs=out_specs, check_vma=False)
```
